256 devices in a mesh: tile: 64 (over z, y, core), chan: 4 (over x).
Axes of the slice: x: 4, y: 4, z: 8, core: 2. Of those that a mesh axis runs over, the one named last changes fastest.
Arguments:
- seq_grad: bfloat16 [73728, 1536], P('tile', 'chan'), may hold values from -6 to 6
- token_slot: int32 [36864], P('tile'), may hold values from 0 to 73727, as said below
- pixels: bfloat16 [36864, 1536], P('tile', 'chan'), may hold values from -6 to 6
- dw_kernel: float32 [49, 1536], P(None, 'chan'), may hold values from -0.875 to 0.875
- ln_gain: float32 [1536], P('chan'), may hold values from 0.5 to 2
- ln_bias: float32 [1536], P('chan'), may hold values from -3 to 3
- w_in: bfloat16 [1536, 6144], P(None, 'chan'), may hold values from -0.15625 to 0.15625
- b_in: float32 [6144], P('chan'), may hold values from -3 to 3
- w_out: bfloat16 [6144, 1536], P('chan'), may hold values from -0.078125 to 0.078125
- layer_scale: float32 [1536], replicated, may hold values from 0.3 to 1.5
Outputs:
- grad_input: bfloat16 [36864, 1536], P('tile', 'chan')
- grad_w_in: float32 [1536, 6144], P('tile', 'chan')
- grad_w_out: float32 [6144, 1536], P('chan', 'tile')
- grad_kernel: float32 [49, 1536], P(None, 'chan')
The draws below stay inside these ranges and needn't reach their ends.
Inputs may be any that keep to these rules, and one draw needn't show every extreme that they name: No two visual tokens name the same slot. Slot s belongs to sequence shard s // 1152. The 576 tokens of one device (an aligned block of token_slot) take at most 18 slots of any one shard, and exactly 18 from some shard in every block.
All inputs are finite; a program needn't handle non-finite values.
Results may differ from the reference program's by a relative error of at most 0.015.
Values may be sent and summed in bfloat16 or wider, within the bound.
No kernel may reach another device: no remote copies, remote signals or barrier semaphores. Data moves between devices by JAX's collectives and lax.ppermute only.
A program may use at most 128 MiB of HBM per device.

```python
import math
import jax
import jax.numpy as jnp
from jax import lax

C = 1536
HID = 6144
KSIZE = 7
PAGE_SIDE = 48
TOK_DEV = 576
TOKENS = 36864
PAGES = 16
CAP = 18
SLOTS = 1152
N_TILE = 64


def draw_token_slot(key, part):
    key = jax.random.fold_in(key, 11)
    seats = N_TILE * CAP
    hot_key, seat_key, order_key, slot_key = jax.random.split(key, 4)
    base = jax.random.randint(hot_key, (), 0, N_TILE)
    offsets = jax.random.randint(jax.random.fold_in(hot_key, 1), (N_TILE,), 0, max(1, N_TILE // 4))
    hot_source = (base + offsets) % N_TILE
    seat_ids = jnp.arange(seats, dtype=jnp.int32)

    def pick(tile_key, hot_one):
        scores = jax.random.permutation(tile_key, seats).astype(jnp.int32)
        scores = jnp.where(seat_ids // CAP == hot_one, scores - seats, scores)
        return jnp.argsort(scores, stable=True)[:TOK_DEV].astype(jnp.int32)
    chosen = jax.vmap(pick)(jax.random.split(seat_key, N_TILE), hot_source)
    shuffle = jax.vmap(lambda one_key: jax.random.permutation(one_key, TOK_DEV))(jax.random.split(order_key, N_TILE))
    chosen = jnp.take_along_axis(chosen, shuffle.astype(jnp.int32), axis=1)
    source = chosen // CAP
    ranks = chosen % CAP
    slot_perm = jax.vmap(lambda one_key: jax.random.permutation(one_key, SLOTS))(jax.random.split(slot_key, N_TILE)).astype(jnp.int32)
    tile_ids = jnp.arange(N_TILE, dtype=jnp.int32)[:, None]
    local_slot = slot_perm[source, tile_ids * CAP + ranks]
    return (source * SLOTS + local_slot).reshape(-1).astype(jnp.int32)


def block_scale(stream_key, shape, pieces, low, largest):
    def one(dim, shards_of):
        steps = jax.random.uniform(jax.random.fold_in(jax.random.fold_in(stream_key, 6), dim), (shards_of,), jnp.float32, low / len(pieces), largest / len(pieces))
        return jnp.repeat(jnp.exp(steps), shape[dim] // shards_of).reshape((-1,) + (1,) * (len(shape) - dim - 1))

    loudness = one(*pieces[0])
    for cut in pieces[1:]:
        loudness = loudness * one(*cut)
    return loudness


def centred(rng, extent, deviation, limit, cuts=(), kind=jnp.bfloat16):
    factor_of = block_scale(rng, extent, cuts, -0.22, 0.18) if cuts else 1.0
    values = jax.random.normal(rng, extent, jnp.float32) * deviation * factor_of
    return jnp.minimum(jnp.maximum(values, -limit), limit).astype(kind)


def setup_inputs(seed: int = 0) -> dict:
    streams_of = jax.random.split(jax.random.key(seed), 11)
    return {
        "seq_grad": centred(streams_of[0], (N_TILE * SLOTS, C), 1.0, 6.0, ((0, 64), (1, 4))),
        "token_slot": draw_token_slot(jax.random.fold_in(streams_of[10], 71), 0),
        "pixels": centred(streams_of[2], (TOKENS, C), 1.0, 6.0, ((0, 64), (1, 4))),
        "dw_kernel": centred(streams_of[3], (KSIZE * KSIZE, C), (KSIZE * KSIZE) ** -0.5, 0.875, ((1, 4),), jnp.float32),
        "ln_gain": jnp.clip(jnp.exp(math.log(2.0) - 1.3862944 * jax.random.uniform(streams_of[4], (C,), jnp.float32) ** block_scale(streams_of[4], (C,), ((0, 4),), -0.2, 0.2)), 0.5, 2.0),
        "ln_bias": centred(streams_of[5], (C,), 0.5, 3.0, ((0, 4),), jnp.float32),
        "w_in": centred(streams_of[6], (C, HID), C ** -0.5, 0.15625, ((1, 4),)),
        "b_in": centred(streams_of[7], (HID,), 0.5, 3.0, ((0, 4),), jnp.float32),
        "w_out": centred(streams_of[8], (HID, C), HID ** -0.5, 0.078125, ((0, 4),)),
        "layer_scale": jnp.clip(jnp.exp(jax.random.uniform(streams_of[9], (C,), jnp.float32, math.log(0.3), math.log(1.5))), 0.3, 1.5),
    }


EPS = 1e-06

def gelu_parts(preact):
    normal_cdf = 0.5 * (1.0 + jax.scipy.special.erf(preact * 0.7071067811865476))
    density = jnp.exp(-0.5 * preact * preact) * 0.3989422804014327
    return (preact * normal_cdf, normal_cdf + preact * density)

def depthwise(padded, kernel, side):
    total = jnp.zeros((padded.shape[0], side, side, padded.shape[3]), jnp.float32)
    for row_off in range(KSIZE):
        for col_off in range(KSIZE):
            window = padded[:, row_off:row_off + side, col_off:col_off + side, :]
            total = total + kernel[row_off * KSIZE + col_off] * window
    return total

def reference(seq_grad, token_slot, pixels, dw_kernel, ln_gain, ln_bias, w_in, b_in, w_out, layer_scale):
    side = PAGE_SIDE
    reach = KSIZE // 2
    upstream = jnp.take(seq_grad, token_slot, axis=0)
    canon = jnp.roll(pixels.astype(jnp.float32), TOK_DEV, axis=0)
    grid = canon.reshape(PAGES, side, side, C)
    padded = jnp.pad(grid, ((0, 0), (reach, reach), (reach, reach), (0, 0)))
    mixed = depthwise(padded, dw_kernel, side).reshape(TOKENS, C)
    center = mixed - lax.optimization_barrier(jnp.mean(mixed, axis=1, keepdims=True))
    inv_std = lax.rsqrt(lax.optimization_barrier(jnp.mean(center * center, axis=1, keepdims=True)) + EPS)
    normed = center * inv_std
    ln_out = (normed * ln_gain + ln_bias).astype(jnp.bfloat16)
    scaled = (upstream.astype(jnp.float32) * layer_scale).astype(jnp.bfloat16)
    scaled = jnp.roll(scaled, TOK_DEV, axis=0)

    def step(carry, inputs):
        acc_in, acc_out = carry
        rows_in, rows_up = inputs
        preact = jnp.dot(rows_in, w_in, preferred_element_type=jnp.float32) + b_in
        act_val, act_slope = gelu_parts(preact)
        hidden = act_val.astype(jnp.bfloat16)
        acc_out = acc_out + jnp.dot(hidden.T, rows_up, preferred_element_type=jnp.float32)
        back_hidden = jnp.dot(rows_up, w_out.T, preferred_element_type=jnp.float32)
        back_pre = (back_hidden * act_slope).astype(jnp.bfloat16)
        acc_in = acc_in + jnp.dot(rows_in.T, back_pre, preferred_element_type=jnp.float32)
        back_norm = jnp.dot(back_pre, w_in.T, preferred_element_type=jnp.float32)
        return ((acc_in, acc_out), back_norm)
    start = (jnp.zeros((C, HID), jnp.float32), jnp.zeros((HID, C), jnp.float32))
    blocks = (ln_out.reshape(PAGES, side * side, C), scaled.reshape(PAGES, side * side, C))
    (acc_in, acc_out), back_norm = lax.scan(step, start, blocks)
    back_norm = back_norm.reshape(TOKENS, C)
    grad_normed = back_norm * ln_gain
    mean_grad = lax.optimization_barrier(jnp.mean(grad_normed, axis=1, keepdims=True))
    mean_cross = lax.optimization_barrier(jnp.mean(grad_normed * normed, axis=1, keepdims=True))
    grad_mixed = inv_std * (grad_normed - mean_grad - normed * mean_cross)
    grad_grid = grad_mixed.reshape(PAGES, side, side, C)
    grad_pad = jnp.pad(grad_grid, ((0, 0), (reach, reach), (reach, reach), (0, 0)))
    back_conv = depthwise(grad_pad, dw_kernel[::-1], side).reshape(TOKENS, C)
    back_conv = jnp.roll(back_conv, -TOK_DEV, axis=0)
    grad_input = (upstream.astype(jnp.float32) + back_conv).astype(jnp.bfloat16)
    taps = []
    for row_off in range(KSIZE):
        for col_off in range(KSIZE):
            window = padded[:, row_off:row_off + side, col_off:col_off + side, :]
            taps.append(lax.optimization_barrier(jnp.sum(window * grad_grid, axis=(0, 1, 2))))
    factor = 1.0 / math.sqrt(TOKENS)
    grad_kernel = jnp.stack(taps) * factor
    return (grad_input, acc_in * factor, acc_out * factor, grad_kernel)
```

```python
import math

import jax
import jax.numpy as jnp
from jax import lax
from jax.sharding import PartitionSpec as P

C = 1536
KSIZE = 7
PAGE_SIDE = 48
EPS = 1e-06
NZ, NY, NCORE, NCHAN = 8, 4, 2, 4
BF16 = jnp.bfloat16
F32 = jnp.float32


def tile_shift(value, dz, dy, dc):
    pairs = []
    for z in range(NZ):
        for y in range(NY):
            for c in range(NCORE):
                source = (z * NY + y) * NCORE + c
                target = ((z + dz) % NZ * NY + (y + dy) % NY) * NCORE + (c + dc) % NCORE
                pairs.append((source, target))
    return lax.ppermute(value, "tile", pairs)


def chan_shift(value, step):
    return lax.ppermute(value, "chan", [(i, (i + step) % NCHAN) for i in range(NCHAN)])


def z_shift(value, step):
    return tile_shift(value, step, 0, 0)


def y_shift(value, step):
    return tile_shift(value, 0, step, 0)


def core_swap(value):
    return tile_shift(value, 0, 0, 1)


def edges(value, width):
    peers = NZ * NY * NCORE
    up = [(i, (i + 1) % peers) for i in range(peers)]
    down = [(j, i) for i, j in up]
    before = lax.ppermute(value[-width:], "tile", up)
    after = lax.ppermute(value[:width], "tile", down)
    return jnp.concatenate([before, value, after], axis=0)


def gelu_parts(preact):
    normal_cdf = 0.5 * (1.0 + jax.scipy.special.erf(preact * 0.7071067811865476))
    density = jnp.exp(-0.5 * preact * preact) * 0.3989422804014327
    return (preact * normal_cdf, normal_cdf + preact * density)


def depthwise(padded, kernel, rows, cols):
    total = jnp.zeros((rows, cols, padded.shape[2]), F32)
    for row_off in range(KSIZE):
        for col_off in range(KSIZE):
            window = padded[row_off : row_off + rows, col_off : col_off + cols, :]
            total = total + kernel[row_off * KSIZE + col_off] * window
    return total


def page_edges(extended, band_index, tiles_page, reach):
    height = extended.shape[0]
    row_ids = lax.broadcasted_iota(jnp.int32, (height, 1, 1), 0)
    first = band_index % tiles_page == 0
    final = band_index % tiles_page == tiles_page - 1
    dropped = (row_ids < reach) & first | (row_ids >= height - reach) & final
    kept = jnp.where(dropped, jnp.zeros_like(extended), extended)
    return jnp.pad(kept, ((0, 0), (reach, reach), (0, 0)))


def meet(get, shift, peers):
    far = peers // 2
    chunk = get(far)
    half = chunk.shape[0] // 2
    up = shift(chunk[:half], 1)
    down = shift(chunk[half:], -1)
    for distance in range(far - 1, 0, -1):
        above = get(distance).astype(F32)
        below = get(-distance).astype(F32)
        if distance == far - 1:
            above = jnp.concatenate([above[:half] + up.astype(F32), above[half:]], axis=0)
            below = jnp.concatenate([below[:half], below[half:] + down.astype(F32)], axis=0)
        else:
            above = above + up.astype(F32)
            below = below + down.astype(F32)
        up = shift(above.astype(BF16), 1)
        down = shift(below.astype(BF16), -1)
    return get(0).astype(F32) + up.astype(F32) + down.astype(F32)


def direct(get, shift, peers):
    parts = [shift(get(k).astype(BF16), k) for k in range(1, peers)]
    total = get(0).astype(F32)
    for part in parts:
        total = total + part.astype(F32)
    return total


def shards(
    seq_grad, token_slot, pixels, dw_kernel, ln_gain, ln_bias, w_in, b_in, w_out, layer_scale
):
    tiles = NZ * NY * NCORE
    position = lax.axis_index("tile")
    chan = lax.axis_index("chan")
    z, y, core = position // (NY * NCORE), position // NCORE % NY, position % NCORE
    band_index = (position + 1) % tiles
    slots = seq_grad.shape[0]
    capacity = slots // tiles
    tok_dev, chan_dev = pixels.shape
    reach = KSIZE // 2
    rows = tok_dev // PAGE_SIDE
    tiles_page = PAGE_SIDE // rows
    factor = 1.0 / math.sqrt(tok_dev * tiles)

    source = token_slot // slots
    local_slot = token_slot % slots
    ids = jnp.arange(tok_dev, dtype=jnp.int32)
    same = (source[:, None] == source[None, :]) & (ids[:, None] < ids[None, :])
    seat = source * capacity + jnp.sum(same.astype(jnp.int32), axis=0)
    seats = jnp.arange(slots, dtype=jnp.int32)
    request = jnp.sum(
        jnp.where(seat[:, None] == seats[None, :], local_slot[:, None] + 1, 0), axis=0
    )
    asked = lax.all_to_all(
        (request - 1).reshape(tiles, capacity), "tile", split_axis=0, concat_axis=0, tiled=True
    ).reshape(slots)
    found = jnp.dot(
        (asked[:, None] == seats[None, :]).astype(BF16), seq_grad, preferred_element_type=F32
    ).astype(BF16)
    arrived = lax.all_to_all(
        found.reshape(tiles, capacity, chan_dev), "tile", split_axis=0, concat_axis=0, tiled=True
    ).reshape(slots, chan_dev)
    upstream = jnp.dot(
        (seat[:, None] == seats[None, :]).astype(BF16), arrived, preferred_element_type=F32
    ).astype(BF16)
    upstream_blocks = [upstream] + [chan_shift(upstream, k) for k in range(1, NCHAN)]

    def turned(value, axis):
        return jnp.concatenate(
            [
                lax.dynamic_slice_in_dim(value, (chan - k) % NCHAN * chan_dev, chan_dev, axis=axis)
                for k in range(NCHAN)
            ],
            axis=axis,
        )

    w_in_t = turned(w_in, 0)
    w_out_t = turned(w_out, 1)
    scale_t = turned(layer_scale, 0)

    grid = pixels.reshape(rows, PAGE_SIDE, chan_dev)
    padded = page_edges(edges(grid, reach).astype(F32), band_index, tiles_page, reach)
    mixed = depthwise(padded, dw_kernel, rows, PAGE_SIDE).reshape(tok_dev, chan_dev)
    own_sum = jnp.sum(mixed, axis=1)
    local = mixed - (own_sum / chan_dev)[:, None]
    own_spread = jnp.sum(local * local, axis=1)
    extra = tok_dev - chan_dev
    message = jnp.stack(
        [own_sum, own_spread, jnp.pad(ln_gain, (0, extra)), jnp.pad(ln_bias, (0, extra))]
    )
    messages = [message] + [chan_shift(message, k) for k in range(1, NCHAN)]
    sent = local.astype(BF16)
    locals_ = [local] + [chan_shift(sent, k) for k in range(1, NCHAN)]
    mean = sum(m[0] for m in messages) / C
    offsets = [m[0] / chan_dev - mean for m in messages]
    spread = sum(m[1] + chan_dev * (d * d) for m, d in zip(messages, offsets))
    inv_std = lax.rsqrt(spread / C + EPS)[:, None]
    gains = [m[2, :chan_dev] for m in messages]
    biases = [m[3, :chan_dev] for m in messages]
    normed = (local + offsets[0][:, None]) * inv_std
    ln_out = jnp.concatenate(
        [
            ((v.astype(F32) + d[:, None]) * inv_std * g + b).astype(BF16)
            for v, d, g, b in zip(locals_, offsets, gains, biases)
        ],
        axis=1,
    )
    gain_t = jnp.concatenate(gains)
    bias_t = jnp.concatenate(biases)
    w_wide = w_in_t.astype(F32)
    gain_w = jnp.sum(gain_t[:, None] * w_wide, axis=0)
    const_w = b_in + jnp.sum(bias_t[:, None] * w_wide, axis=0)

    preact = jnp.dot(ln_out, w_in_t, preferred_element_type=F32) + b_in
    act_val, act_slope = gelu_parts(preact)
    hidden = act_val.astype(BF16)
    scaled = (
        jnp.concatenate(upstream_blocks, axis=1).astype(F32) * scale_t
    ).astype(BF16)
    back_hidden = lax.dot_general(
        scaled, w_out_t, (((1,), (1,)), ((), ())), preferred_element_type=F32
    )
    back_pre = (back_hidden * act_slope).astype(BF16)
    back_wide = back_pre.astype(F32)
    cross = jnp.stack(
        [
            jnp.sum(back_wide * gain_w, axis=1),
            jnp.sum(back_wide * (preact - const_w), axis=1),
        ]
    )
    crosses = [cross] + [chan_shift(cross, k) for k in range(1, NCHAN)]

    def share(k):
        block = (NCHAN - k) % NCHAN
        weights = w_in_t[block * chan_dev : (block + 1) * chan_dev]
        return lax.dot_general(
            back_pre, weights, (((1,), (1,)), ((), ())), preferred_element_type=F32
        )

    back_parts = [chan_shift(share(k).astype(BF16), k) for k in (2, 1, 3)]

    def halved(partial):
        whole = (partial * factor).reshape(NZ * NY, NCORE, -1, partial.shape[1])
        theirs = lax.dynamic_index_in_dim(whole, 1 - core, 1, keepdims=False).astype(BF16)
        ours = lax.dynamic_index_in_dim(whole, core, 1, keepdims=False)
        kept = (ours + core_swap(theirs).astype(F32)).astype(BF16)
        return kept.reshape(NZ, NY, *kept.shape[1:])

    def z_place(k):
        at = (z + k) % NZ
        return (chan - at // 2) % NCHAN * 2 + at % 2

    out_half = halved(
        lax.dot_general(scaled, hidden, (((0,), (0,)), ((), ())), preferred_element_type=F32)
    )
    out_y = meet(
        lambda k: lax.dynamic_index_in_dim(out_half, z_place(k), 0, keepdims=False), z_shift, NZ
    )
    grad_w_out = direct(
        lambda k: lax.dynamic_index_in_dim(out_y, (y + k) % NY, 0, keepdims=False), y_shift, NY
    ).T

    in_half = halved(
        lax.dot_general(ln_out, back_pre, (((0,), (0,)), ((), ())), preferred_element_type=F32)
    )
    in_z = meet(
        lambda k: lax.dynamic_index_in_dim(in_half, (y + k) % NY, 1, keepdims=False), y_shift, NY
    )
    grad_w_in = direct(
        lambda k: lax.dynamic_index_in_dim(in_z, z_place(k), 0, keepdims=False), z_shift, NZ
    )

    back_norm = share(0)
    for part in back_parts:
        back_norm = back_norm + part.astype(F32)
    grad_normed = back_norm * ln_gain
    cross_sum = sum(crosses)
    sum_grad, sum_cross = cross_sum[0], cross_sum[1]
    grad_mixed = inv_std * (
        grad_normed - (sum_grad / C)[:, None] - normed * (sum_cross / C)[:, None]
    )
    grad_grid = grad_mixed.reshape(rows, PAGE_SIDE, chan_dev)
    grad_ext = edges(grad_grid.astype(BF16), reach).astype(F32)
    grad_pad = page_edges(grad_ext, band_index, tiles_page, reach)
    back_conv = depthwise(grad_pad, dw_kernel[::-1], rows, PAGE_SIDE).reshape(tok_dev, chan_dev)
    grad_input = (upstream.astype(F32) + back_conv).astype(BF16)
    taps = []
    for row_off in range(KSIZE):
        for col_off in range(KSIZE):
            window = padded[row_off : row_off + rows, col_off : col_off + PAGE_SIDE, :]
            taps.append(jnp.sum(window * grad_grid, axis=(0, 1)))
    taps = jnp.stack(taps) * factor
    taps = taps + core_swap(taps)

    def all_sum(value, shift, here, peers):
        stack = jnp.stack([value] + [shift(value, k) for k in range(1, peers)])
        total = jnp.zeros(value.shape, F32)
        for peer in range(peers):
            total = total + lax.dynamic_index_in_dim(
                stack, (here - peer) % peers, 0, keepdims=False
            ).astype(F32)
        return total

    taps = all_sum(taps, y_shift, y, NY)
    grad_kernel = all_sum(taps.astype(BF16), z_shift, z, NZ)
    return (grad_input, grad_w_in, grad_w_out, grad_kernel)


def solution(mesh):
    placed = (
        P("tile", "chan"),
        P("tile"),
        P("tile", "chan"),
        P(None, "chan"),
        P("chan"),
        P("chan"),
        P(None, "chan"),
        P("chan"),
        P("chan", None),
        P(),
    )
    return jax.shard_map(
        shards,
        mesh=mesh,
        in_specs=placed,
        out_specs=(P("tile", "chan"), P("tile", "chan"), P("chan", "tile"), P(None, "chan")),
        check_vma=False,
    )
```

```python
import functools
import math

import jax
import jax.numpy as jnp
from jax import lax
from jax.experimental import pallas as pl
from jax.experimental.pallas import tpu as pltpu
from jax.sharding import PartitionSpec as P

C = 1536
KSIZE = 7
PAGE_SIDE = 48
EPS = 1e-06
NZ, NY, NCORE, NCHAN = 8, 4, 2, 4
BF16 = jnp.bfloat16
F32 = jnp.float32


def tile_shift(value, dz, dy, dc):
    pairs = []
    for z in range(NZ):
        for y in range(NY):
            for c in range(NCORE):
                source = (z * NY + y) * NCORE + c
                target = ((z + dz) % NZ * NY + (y + dy) % NY) * NCORE + (c + dc) % NCORE
                pairs.append((source, target))
    return lax.ppermute(value, "tile", pairs)


def chan_shift(value, step):
    return lax.ppermute(value, "chan", [(i, (i + step) % NCHAN) for i in range(NCHAN)])


def z_shift(value, step):
    return tile_shift(value, step, 0, 0)


def y_shift(value, step):
    return tile_shift(value, 0, step, 0)


def core_swap(value):
    return tile_shift(value, 0, 0, 1)


def edges(value, width):
    peers = NZ * NY * NCORE
    up = [(i, (i + 1) % peers) for i in range(peers)]
    down = [(j, i) for i, j in up]
    before = lax.ppermute(value[-width:], "tile", up)
    after = lax.ppermute(value[:width], "tile", down)
    return before, value, after


def gelu_parts(preact):
    normal_cdf = 0.5 * (1.0 + jax.scipy.special.erf(preact * 0.7071067811865476))
    density = jnp.exp(-0.5 * preact * preact) * 0.3989422804014327
    return (preact * normal_cdf, normal_cdf + preact * density)


LANES = 128
MARGIN = 8


def stage_windows(flags_ref, before_ref, own_ref, after_ref, pad, shifted):
    rows, cols, reach = own_ref.shape[0], own_ref.shape[1], KSIZE // 2
    pad[:, :MARGIN] = jnp.zeros((pad.shape[0], MARGIN, LANES), F32)
    pad[:, MARGIN + cols :] = jnp.zeros((pad.shape[0], MARGIN, LANES), F32)
    inside = slice(MARGIN, MARGIN + cols)
    pad[:reach, inside] = jnp.where(flags_ref[0] == 1, 0.0, before_ref[...].astype(F32))
    pad[reach : reach + rows, inside] = own_ref[...].astype(F32)
    pad[reach + rows :, inside] = jnp.where(flags_ref[1] == 1, 0.0, after_ref[...].astype(F32))
    for col_off in range(KSIZE):
        start = MARGIN - reach + col_off
        shifted[col_off] = pad[:, start : start + cols]


def conv_kernel(flags_ref, before_ref, own_ref, after_ref, taps_ref, *rest, flipped):
    *extra, out_ref, pad, shifted = rest
    stage_windows(flags_ref, before_ref, own_ref, after_ref, pad, shifted)
    rows, cols = own_ref.shape[0], own_ref.shape[1]
    group = 4

    def body(index, carry):
        first = index * group
        sums = [jnp.zeros((cols, LANES), F32)] * group
        for col_off in range(KSIZE):
            for line in range(group + KSIZE - 1):
                window = shifted[col_off, first + line]
                for row in range(group):
                    row_off = line - row
                    if 0 <= row_off < KSIZE:
                        tap = row_off * KSIZE + col_off
                        tap = KSIZE * KSIZE - 1 - tap if flipped else tap
                        sums[row] = sums[row] + taps_ref[tap : tap + 1, :] * window
        for row in range(group):
            value = sums[row]
            for ref in extra:
                value = value + ref[first + row].astype(F32)
            out_ref[first + row] = value.astype(out_ref.dtype)
        return carry

    lax.fori_loop(0, rows // group, body, 0)


def taps_kernel(flags_ref, before_ref, own_ref, after_ref, grad_ref, out_ref, pad, shifted, held, *, factor):
    stage_windows(flags_ref, before_ref, own_ref, after_ref, pad, shifted)
    rows, cols = own_ref.shape[0], own_ref.shape[1]
    group = 2
    held[...] = jnp.zeros(held.shape, F32)

    def body(index, carry):
        first = index * group
        grads = [grad_ref[first + row] for row in range(group)]
        for row_off in range(KSIZE):
            for col_off in range(KSIZE):
                value = shifted[col_off, first + row_off] * grads[0]
                for row in range(1, group):
                    value = value + shifted[col_off, first + row + row_off] * grads[row]
                tap = row_off * KSIZE + col_off
                held[tap] = held[tap] + jnp.sum(value.reshape(cols // 8, 8, LANES), axis=0)
        return carry

    lax.fori_loop(0, rows // group, body, 0)
    out_ref[...] = jnp.sum(held[...], axis=1) * factor


def banded(kernel, flags, band, others, out_shape, scratch=()):
    before, own, after_rows = band

    def spec(shape):
        index = (0,) * (len(shape) - 1)
        return pl.BlockSpec(shape[:-1] + (LANES,), lambda i: index + (i,))

    rows, cols, width = own.shape
    height = rows + 2 * (KSIZE // 2)
    return pl.pallas_call(
        kernel,
        out_shape=out_shape,
        grid=(width // LANES,),
        in_specs=[pl.BlockSpec(memory_space=pltpu.SMEM)]
        + [spec(v.shape) for v in (before, own, after_rows, *others)],
        out_specs=spec(out_shape.shape),
        scratch_shapes=[
            pltpu.VMEM((height, cols + 2 * MARGIN, LANES), F32),
            pltpu.VMEM((KSIZE, height, cols, LANES), F32),
            *scratch,
        ],
        compiler_params=pltpu.CompilerParams(vmem_limit_bytes=32 * 1024 * 1024),
        cost_estimate=pl.CostEstimate(flops=1000, bytes_accessed=1000, transcendentals=0),
    )(flags, before, own, after_rows, *others)


def direct(get, shift, peers):
    parts = [shift(get(k).astype(BF16), k) for k in range(1, peers)]
    total = get(0).astype(F32)
    for part in parts:
        total = total + part.astype(F32)
    return total


def tie(*values):
    return lax.optimization_barrier(values)


def thirds(value):
    high = lax.reduce_precision(value, 8, 7)
    middle = lax.reduce_precision(value - high, 8, 7)
    low = value - high - middle
    return jnp.concatenate([high, middle, low], axis=0).astype(BF16)


def joined(parts):
    rows = parts.shape[0] // 3
    high, middle, low = (parts[i * rows : (i + 1) * rows].astype(F32) for i in range(3))
    return high + (middle + low)


def joined_products(parts, weights):
    return joined(jnp.dot(parts, weights, preferred_element_type=F32))


def pick(value, index, axis):
    return lax.dynamic_index_in_dim(
        value, index, axis, keepdims=False, allow_negative_indices=False
    )


def shards(
    seq_grad, token_slot, pixels, dw_kernel, ln_gain, ln_bias, w_in, b_in, w_out, layer_scale
):
    tiles = NZ * NY * NCORE
    position = lax.axis_index("tile")
    chan = lax.axis_index("chan")
    z, y = position >> 3, (position >> 1) & (NY - 1)
    band_index = (position + 1) & (tiles - 1)
    slots = seq_grad.shape[0]
    capacity = slots // tiles
    tok_dev, chan_dev = pixels.shape
    reach = KSIZE // 2
    rows = tok_dev // PAGE_SIDE
    page_part = band_index & (PAGE_SIDE // rows - 1)
    flags = jnp.stack([page_part == 0, page_part == PAGE_SIDE // rows - 1]).astype(jnp.int32)
    factor = 1.0 / math.sqrt(tok_dev * tiles)

    band = edges(pixels.reshape(rows, PAGE_SIDE, chan_dev), reach)
    source = token_slot // slots
    local_slot = token_slot - source * slots
    ids = jnp.arange(tok_dev, dtype=jnp.int32)
    same = (source[:, None] == source[None, :]) & (ids[:, None] < ids[None, :])
    seat = source * capacity + jnp.sum(same.astype(jnp.int32), axis=0)
    seats = jnp.arange(slots, dtype=jnp.int32)
    request = jnp.sum(
        jnp.where(seat[:, None] == seats[None, :], local_slot[:, None] + 1, 0), axis=0
    )
    asked = lax.all_to_all(
        (request - 1).reshape(tiles, capacity), "tile", split_axis=0, concat_axis=0, tiled=True
    ).reshape(slots)
    found = jnp.dot(
        (asked[:, None] == seats[None, :]).astype(BF16), seq_grad, preferred_element_type=F32
    ).astype(BF16)
    found, *band = tie(found, *band)
    arrived = lax.all_to_all(
        found.reshape(tiles, capacity * 3, chan_dev // 3),
        "tile",
        split_axis=0,
        concat_axis=0,
        tiled=True,
    ).reshape(slots, chan_dev)

    mixed = banded(
        functools.partial(conv_kernel, flipped=False),
        flags,
        band,
        (dw_kernel,),
        jax.ShapeDtypeStruct((rows, PAGE_SIDE, chan_dev), F32),
    ).reshape(tok_dev, chan_dev)
    own_sum = jnp.sum(mixed, axis=1)
    local = mixed - (own_sum / chan_dev)[:, None]
    own_spread = jnp.sum(local * local, axis=1)
    extra = tok_dev - chan_dev
    message = jnp.stack(
        [own_sum, own_spread, jnp.pad(ln_gain, (0, extra)), jnp.pad(ln_bias, (0, extra))]
    )
    packed = thirds(message).reshape(-1, chan_dev)
    sent = jnp.concatenate([local.astype(BF16), packed], axis=0)
    received = [chan_shift(sent, k) for k in range(1, NCHAN)]

    upstream = jnp.dot(
        (seat[:, None] == seats[None, :]).astype(BF16), arrived, preferred_element_type=F32
    ).astype(BF16)
    upstream, w_in, w_out = tie(upstream, w_in, w_out)
    upstream_blocks = [upstream] + [chan_shift(upstream, k) for k in range(1, NCHAN)]

    def turned(value, axis):
        return jnp.concatenate(
            [
                lax.dynamic_slice_in_dim(
                    value,
                    ((chan - k) & (NCHAN - 1)) * chan_dev,
                    chan_dev,
                    axis=axis,
                    allow_negative_indices=False,
                )
                for k in range(NCHAN)
            ],
            axis=axis,
        )

    w_in_t = turned(w_in, 0)
    scale_t = turned(layer_scale, 0)

    locals_ = [local] + [r[:tok_dev] for r in received]
    messages = [message] + [
        joined(r[tok_dev:].reshape(3 * message.shape[0], -1)) for r in received
    ]
    mean = sum(m[0] for m in messages) / C
    offsets = [m[0] / chan_dev - mean for m in messages]
    spread = sum(m[1] + chan_dev * (d * d) for m, d in zip(messages, offsets))
    inv_std = lax.rsqrt(spread / C + EPS)[:, None]
    gains = [m[2, :chan_dev] for m in messages]
    biases = [m[3, :chan_dev] for m in messages]
    normed = (local + offsets[0][:, None]) * inv_std
    ln_out = jnp.concatenate(
        [
            ((v.astype(F32) + d[:, None]) * inv_std * g + b).astype(BF16)
            for v, d, g, b in zip(locals_, offsets, gains, biases)
        ],
        axis=1,
    )
    preact = jnp.dot(ln_out, w_in_t, preferred_element_type=F32) + b_in
    act_val, act_slope = gelu_parts(preact)
    hidden = act_val.astype(BF16)
    w_out_t = turned(w_out, 1)
    vectors = jnp.stack([jnp.concatenate(gains), jnp.concatenate(biases)])
    vectors_w = joined_products(thirds(vectors), w_in_t)
    gain_w, const_w = vectors_w[0], vectors_w[1] + b_in

    hidden, gain_w, const_w, w_out_t, *upstream_blocks = tie(
        hidden, gain_w, const_w, w_out_t, *upstream_blocks
    )
    scaled = (
        jnp.concatenate(upstream_blocks, axis=1).astype(F32) * scale_t
    ).astype(BF16)
    back_hidden = lax.dot_general(
        scaled, w_out_t, (((1,), (1,)), ((), ())), preferred_element_type=F32
    )
    back_pre = (back_hidden * act_slope).astype(BF16)
    back_wide = back_pre.astype(F32)
    cross = jnp.stack(
        [
            jnp.sum(back_wide * gain_w, axis=1),
            jnp.sum(back_wide * (preact - const_w), axis=1),
        ]
    )
    crosses = [cross] + [chan_shift(cross, k) for k in range(1, NCHAN)]

    def share(k, values):
        block = (NCHAN - k) % NCHAN
        weights = w_in_t[block * chan_dev : (block + 1) * chan_dev]
        return lax.dot_general(
            values, weights, (((1,), (1,)), ((), ())), preferred_element_type=F32
        )

    core = position & (NCORE - 1)

    def weight_grad(left, right):
        grad = lax.dot_general(
            left, right, (((0,), (0,)), ((), ())), preferred_element_type=F32
        )
        return (grad * factor).astype(BF16).reshape(NZ * NY, NCORE, -1, right.shape[1])

    grad_in = weight_grad(ln_out, back_pre)
    hidden, in_theirs, *crosses = tie(hidden, pick(grad_in, 1 - core, 1), *crosses)
    in_arrived = core_swap(in_theirs)
    grad_out = weight_grad(scaled, hidden)
    back_pre, out_theirs = tie(back_pre, pick(grad_out, 1 - core, 1))
    out_arrived = core_swap(out_theirs)

    shares = [share(k, back_pre).astype(BF16) for k in (2, 1, 3)]
    back_pre, *shares = tie(back_pre, *shares)
    back_parts = [chan_shift(s, k) for s, k in zip(shares, (2, 1, 3))]
    back_own = share(0, back_pre)

    in_arrived, out_arrived, back_own = tie(in_arrived, out_arrived, back_own)
    kept = jnp.stack(
        [
            (pick(grad_in, core, 1).astype(F32) + in_arrived.astype(F32)).astype(BF16),
            (pick(grad_out, core, 1).astype(F32) + out_arrived.astype(F32)).astype(BF16),
        ]
    )
    kept = kept.reshape(2, NZ, NY, *kept.shape[2:])

    def get(k):
        at = (z + k) & (NZ - 1)
        return pick(kept, ((chan - (at >> 1)) & (NCHAN - 1)) * 2 + (at & 1), 1)

    far = NZ // 2
    chunk, kept, back_own = tie(get(far), kept, back_own)
    up = z_shift(chunk[:1], 1)
    down = z_shift(chunk[1:], -1)

    def ring_step(distance, up, down):
        above = get(distance).astype(F32)
        below = get(-distance).astype(F32)
        if distance == far - 1:
            above = jnp.concatenate([above[:1] + up.astype(F32), above[1:]], axis=0)
            below = jnp.concatenate([below[:1], below[1:] + down.astype(F32)], axis=0)
        else:
            above = above + up.astype(F32)
            below = below + down.astype(F32)
        return above.astype(BF16), below.astype(BF16)

    above, below = ring_step(3, up, down)
    above, below, back_own = tie(above, below, back_own)
    up, down = z_shift(above, 1), z_shift(below, -1)


    back_norm = back_own
    for part in back_parts:
        back_norm = back_norm + part.astype(F32)
    grad_normed = back_norm * ln_gain
    cross_sum = sum(crosses)
    sum_grad, sum_cross = cross_sum[0], cross_sum[1]
    grad_mixed = inv_std * (
        grad_normed - (sum_grad / C)[:, None] - normed * (sum_cross / C)[:, None]
    )
    grad_grid = grad_mixed.reshape(rows, PAGE_SIDE, chan_dev)

    before, _, behind = edges(grad_grid.astype(BF16), reach)
    taps = banded(
        functools.partial(taps_kernel, factor=factor),
        flags,
        band,
        (grad_grid,),
        jax.ShapeDtypeStruct((KSIZE * KSIZE, chan_dev), F32),
        (pltpu.VMEM((KSIZE * KSIZE, 8, LANES), F32),),
    )

    def flip(axis, mask):
        pairs = []
        for zz in range(NZ):
            for yy in range(NY):
                for cc in range(NCORE):
                    mate = {
                        "z": (zz ^ mask, yy, cc), "y": (zz, yy ^ mask, cc), "c": (zz, yy, cc ^ mask)
                    }[axis]
                    pairs.append(
                        ((zz * NY + yy) * NCORE + cc, (mate[0] * NY + mate[1]) * NCORE + mate[2])
                    )
        return pairs

    def both(value, axis, mask):
        rounded = lax.reduce_precision(value, 8, 7)
        return rounded + lax.ppermute(rounded.astype(BF16), "tile", flip(axis, mask)).astype(F32)

    taps = taps + core_swap(taps)
    taps = both(taps, "y", 1)
    up, down, taps = tie(up, down, taps)
    above, below = ring_step(2, up, down)
    above, below, taps, before, behind = tie(above, below, taps, before, behind)
    up, down = z_shift(above, 1), z_shift(below, -1)
    grad_input = banded(
        functools.partial(conv_kernel, flipped=True),
        flags,
        (before, grad_grid, behind),
        (dw_kernel, upstream.reshape(rows, PAGE_SIDE, chan_dev)),
        jax.ShapeDtypeStruct((rows, PAGE_SIDE, chan_dev), BF16),
    ).reshape(tok_dev, chan_dev)
    taps = both(taps, "y", 2)
    up, down, taps, grad_input = tie(up, down, taps, grad_input)
    above, below = ring_step(1, up, down)
    above, below, taps = tie(above, below, taps)
    up, down = z_shift(above, 1), z_shift(below, -1)
    taps = both(taps, "z", 1)
    up, down, taps = tie(up, down, taps)
    summed = get(0).astype(F32) + up.astype(F32) + down.astype(F32)
    grads = direct(lambda k: pick(summed, (y + k) & (NY - 1), 1), y_shift, NY)
    grad_w_in, grad_w_out = grads[0], grads[1].T
    taps = both(taps, "z", 2)
    grad_kernel = both(taps, "z", 4)
    return (grad_input, grad_w_in, grad_w_out, grad_kernel)


def solution(mesh):
    placed = (
        P("tile", "chan"),
        P("tile"),
        P("tile", "chan"),
        P(None, "chan"),
        P("chan"),
        P("chan"),
        P(None, "chan"),
        P("chan"),
        P("chan", None),
        P(),
    )
    return jax.shard_map(
        shards,
        mesh=mesh,
        in_specs=placed,
        out_specs=(P("tile", "chan"), P("tile", "chan"), P("chan", "tile"), P(None, "chan")),
        check_vma=False,
    )
```

```python
import functools
import math

import jax
import jax.numpy as jnp
from jax import lax
from jax.experimental import pallas as pl
from jax.experimental.pallas import tpu as pltpu
from jax.sharding import PartitionSpec as P

C = 1536
KSIZE = 7
PAGE_SIDE = 48
EPS = 1e-06
NZ, NY, NCORE, NCHAN = 8, 4, 2, 4
BF16 = jnp.bfloat16
F32 = jnp.float32


def tile_shift(value, dz, dy, dc):
    pairs = []
    for z in range(NZ):
        for y in range(NY):
            for c in range(NCORE):
                source = (z * NY + y) * NCORE + c
                target = ((z + dz) % NZ * NY + (y + dy) % NY) * NCORE + (c + dc) % NCORE
                pairs.append((source, target))
    return lax.ppermute(value, "tile", pairs)


def chan_shift(value, step):
    return lax.ppermute(value, "chan", [(i, (i + step) % NCHAN) for i in range(NCHAN)])


def z_shift(value, step):
    return tile_shift(value, step, 0, 0)


def y_shift(value, step):
    return tile_shift(value, 0, step, 0)


def core_swap(value):
    return tile_shift(value, 0, 0, 1)


def edges(value, width):
    peers = NZ * NY * NCORE
    up = [(i, (i + 1) % peers) for i in range(peers)]
    down = [(j, i) for i, j in up]
    before = lax.ppermute(value[-width:], "tile", up)
    after = lax.ppermute(value[:width], "tile", down)
    return before, value, after


def gelu_parts(preact):
    normal_cdf = 0.5 * (1.0 + jax.scipy.special.erf(preact * 0.7071067811865476))
    density = jnp.exp(-0.5 * preact * preact) * 0.3989422804014327
    return (preact * normal_cdf, normal_cdf + preact * density)


LANES = 128
MARGIN = 8


def stage_windows(flags_ref, before_ref, own_ref, after_ref, pad, shifted):
    rows, cols, reach = own_ref.shape[0], own_ref.shape[1], KSIZE // 2
    pad[:, :MARGIN] = jnp.zeros((pad.shape[0], MARGIN, LANES), F32)
    pad[:, MARGIN + cols :] = jnp.zeros((pad.shape[0], MARGIN, LANES), F32)
    inside = slice(MARGIN, MARGIN + cols)
    pad[:reach, inside] = jnp.where(flags_ref[0] == 1, 0.0, before_ref[...].astype(F32))
    pad[reach : reach + rows, inside] = own_ref[...].astype(F32)
    pad[reach + rows :, inside] = jnp.where(flags_ref[1] == 1, 0.0, after_ref[...].astype(F32))
    for col_off in range(KSIZE):
        start = MARGIN - reach + col_off
        shifted[col_off] = pad[:, start : start + cols]


def conv_kernel(flags_ref, before_ref, own_ref, after_ref, taps_ref, *rest, flipped):
    *extra, out_ref, pad, shifted = rest
    stage_windows(flags_ref, before_ref, own_ref, after_ref, pad, shifted)
    rows, cols = own_ref.shape[0], own_ref.shape[1]
    group = 4

    def body(index, carry):
        first = index * group
        sums = [jnp.zeros((cols, LANES), F32)] * group
        for col_off in range(KSIZE):
            for line in range(group + KSIZE - 1):
                window = shifted[col_off, first + line]
                for row in range(group):
                    row_off = line - row
                    if 0 <= row_off < KSIZE:
                        tap = row_off * KSIZE + col_off
                        tap = KSIZE * KSIZE - 1 - tap if flipped else tap
                        sums[row] = sums[row] + taps_ref[tap : tap + 1, :] * window
        for row in range(group):
            value = sums[row]
            for ref in extra:
                value = value + ref[first + row].astype(F32)
            out_ref[first + row] = value.astype(out_ref.dtype)
        return carry

    lax.fori_loop(0, rows // group, body, 0)


def taps_kernel(flags_ref, before_ref, own_ref, after_ref, grad_ref, out_ref, pad, shifted, held, *, factor):
    stage_windows(flags_ref, before_ref, own_ref, after_ref, pad, shifted)
    rows, cols = own_ref.shape[0], own_ref.shape[1]
    group = 2
    held[...] = jnp.zeros(held.shape, F32)

    def body(index, carry):
        first = index * group
        grads = [grad_ref[first + row] for row in range(group)]
        for row_off in range(KSIZE):
            for col_off in range(KSIZE):
                value = shifted[col_off, first + row_off] * grads[0]
                for row in range(1, group):
                    value = value + shifted[col_off, first + row + row_off] * grads[row]
                tap = row_off * KSIZE + col_off
                held[tap] = held[tap] + jnp.sum(value.reshape(cols // 8, 8, LANES), axis=0)
        return carry

    lax.fori_loop(0, rows // group, body, 0)
    out_ref[...] = jnp.sum(held[...], axis=1) * factor


def banded(kernel, flags, band, others, out_shape, scratch=()):
    before, own, after_rows = band

    def spec(shape):
        index = (0,) * (len(shape) - 1)
        return pl.BlockSpec(shape[:-1] + (LANES,), lambda i: index + (i,))

    rows, cols, width = own.shape
    height = rows + 2 * (KSIZE // 2)
    return pl.pallas_call(
        kernel,
        out_shape=out_shape,
        grid=(width // LANES,),
        in_specs=[pl.BlockSpec(memory_space=pltpu.SMEM)]
        + [spec(v.shape) for v in (before, own, after_rows, *others)],
        out_specs=spec(out_shape.shape),
        scratch_shapes=[
            pltpu.VMEM((height, cols + 2 * MARGIN, LANES), F32),
            pltpu.VMEM((KSIZE, height, cols, LANES), F32),
            *scratch,
        ],
        compiler_params=pltpu.CompilerParams(vmem_limit_bytes=32 * 1024 * 1024),
        cost_estimate=pl.CostEstimate(flops=1000, bytes_accessed=1000, transcendentals=0),
    )(flags, before, own, after_rows, *others)


def tie(*values):
    return lax.optimization_barrier(values)


def thirds(value):
    high = lax.reduce_precision(value, 8, 7)
    middle = lax.reduce_precision(value - high, 8, 7)
    low = value - high - middle
    return jnp.concatenate([high, middle, low], axis=0).astype(BF16)


def joined(parts):
    rows = parts.shape[0] // 3
    high, middle, low = (parts[i * rows : (i + 1) * rows].astype(F32) for i in range(3))
    return high + (middle + low)


def joined_products(parts, weights):
    return joined(jnp.dot(parts, weights, preferred_element_type=F32))


def pick(value, index, axis):
    return lax.dynamic_index_in_dim(
        value, index, axis, keepdims=False, allow_negative_indices=False
    )


def grads_kernel(left_ref, right_ref, ours_ref, theirs_ref, *, factor, rows):
    core = lax.axis_index("tile") & (NCORE - 1)
    grad = factor * lax.dot_general(
        left_ref[...], right_ref[...], (((0,), (0,)), ((), ())), preferred_element_type=F32
    )
    grad = grad.reshape(-1, NCORE, rows, grad.shape[1])
    first, second = grad[:, 0].reshape(ours_ref.shape), grad[:, 1].reshape(ours_ref.shape)
    ours_ref[...] = jnp.where(core == 0, first, second).astype(BF16)
    theirs_ref[...] = jnp.where(core == 0, second, first).astype(BF16)


def weight_grad(left, right, factor):
    tokens, width = left.shape
    block = width // NCHAN
    rows = width // (NZ * NY * NCORE)
    out = jax.ShapeDtypeStruct((width // NCORE, width), BF16)
    half = pl.BlockSpec((block // NCORE, width), lambda i: (i, 0))
    return pl.pallas_call(
        functools.partial(grads_kernel, factor=factor, rows=rows),
        out_shape=(out, out),
        grid=(NCHAN,),
        in_specs=[
            pl.BlockSpec((tokens, block), lambda i: (0, i)),
            pl.BlockSpec((tokens, width), lambda i: (0, 0)),
        ],
        out_specs=(half, half),
        compiler_params=pltpu.CompilerParams(vmem_limit_bytes=32 * 1024 * 1024),
        cost_estimate=pl.CostEstimate(flops=1000, bytes_accessed=1000, transcendentals=0),
    )(left, right)


def shards(
    seq_grad, token_slot, pixels, dw_kernel, ln_gain, ln_bias, w_in, b_in, w_out, layer_scale
):
    tiles = NZ * NY * NCORE
    position = lax.axis_index("tile")
    chan = lax.axis_index("chan")
    z, y = position >> 3, (position >> 1) & (NY - 1)
    band_index = (position + 1) & (tiles - 1)
    slots = seq_grad.shape[0]
    capacity = slots // tiles
    tok_dev, chan_dev = pixels.shape
    reach = KSIZE // 2
    rows = tok_dev // PAGE_SIDE
    page_part = band_index & (PAGE_SIDE // rows - 1)
    flags = jnp.stack([page_part == 0, page_part == PAGE_SIDE // rows - 1]).astype(jnp.int32)
    factor = 1.0 / math.sqrt(tok_dev * tiles)

    band = edges(pixels.reshape(rows, PAGE_SIDE, chan_dev), reach)
    source = token_slot // slots
    local_slot = token_slot - source * slots
    ids = jnp.arange(tok_dev, dtype=jnp.int32)
    same = (source[:, None] == source[None, :]) & (ids[:, None] < ids[None, :])
    seat = source * capacity + jnp.sum(same.astype(jnp.int32), axis=0)
    seats = jnp.arange(slots, dtype=jnp.int32)
    request = jnp.sum(
        jnp.where(seat[:, None] == seats[None, :], local_slot[:, None] + 1, 0), axis=0
    )
    asked = lax.all_to_all(
        (request - 1).reshape(tiles, capacity), "tile", split_axis=0, concat_axis=0, tiled=True
    ).reshape(slots)
    found = jnp.dot(
        (asked[:, None] == seats[None, :]).astype(BF16), seq_grad, preferred_element_type=F32
    ).astype(BF16)
    found, *band = tie(found, *band)
    arrived = lax.all_to_all(
        found.reshape(tiles, capacity * 3, chan_dev // 3),
        "tile",
        split_axis=0,
        concat_axis=0,
        tiled=True,
    ).reshape(slots, chan_dev)

    mixed = banded(
        functools.partial(conv_kernel, flipped=False),
        flags,
        band,
        (dw_kernel,),
        jax.ShapeDtypeStruct((rows, PAGE_SIDE, chan_dev), F32),
    ).reshape(tok_dev, chan_dev)
    own_sum = jnp.sum(mixed, axis=1)
    local = mixed - (own_sum / chan_dev)[:, None]
    own_spread = jnp.sum(local * local, axis=1)
    extra = tok_dev - chan_dev
    message = jnp.stack(
        [own_sum, own_spread, jnp.pad(ln_gain, (0, extra)), jnp.pad(ln_bias, (0, extra))]
    )
    packed = thirds(message).reshape(-1, chan_dev)
    sent = jnp.concatenate([local.astype(BF16), packed], axis=0)
    received = [chan_shift(sent, k) for k in range(1, NCHAN)]

    upstream = jnp.dot(
        (seat[:, None] == seats[None, :]).astype(BF16), arrived, preferred_element_type=F32
    ).astype(BF16)
    upstream, w_in, w_out = tie(upstream, w_in, w_out)
    upstream_blocks = [chan_shift(upstream, k) for k in range(1, NCHAN)]
    upstream, *received = tie(upstream, *received)
    upstream_blocks = [upstream] + upstream_blocks

    def turned(value, axis):
        return jnp.concatenate(
            [
                lax.dynamic_slice_in_dim(
                    value,
                    ((chan - k) & (NCHAN - 1)) * chan_dev,
                    chan_dev,
                    axis=axis,
                    allow_negative_indices=False,
                )
                for k in range(NCHAN)
            ],
            axis=axis,
        )

    w_in_t = turned(w_in, 0)
    scale_t = turned(layer_scale, 0)

    locals_ = [local] + [r[:tok_dev] for r in received]
    messages = [message] + [
        joined(r[tok_dev:].reshape(3 * message.shape[0], -1)) for r in received
    ]
    mean = sum(m[0] for m in messages) / C
    offsets = [m[0] / chan_dev - mean for m in messages]
    spread = sum(m[1] + chan_dev * (d * d) for m, d in zip(messages, offsets))
    inv_std = lax.rsqrt(spread / C + EPS)[:, None]
    gains = [m[2, :chan_dev] for m in messages]
    biases = [m[3, :chan_dev] for m in messages]
    normed = (local + offsets[0][:, None]) * inv_std
    ln_out = jnp.concatenate(
        [
            ((v.astype(F32) + d[:, None]) * inv_std * g + b).astype(BF16)
            for v, d, g, b in zip(locals_, offsets, gains, biases)
        ],
        axis=1,
    )
    preact = jnp.dot(ln_out, w_in_t, preferred_element_type=F32) + b_in
    act_val, act_slope = gelu_parts(preact)
    hidden = act_val.astype(BF16)
    w_out_t = turned(w_out, 1)
    vectors = jnp.stack([jnp.concatenate(gains), jnp.concatenate(biases)])
    vectors_w = joined_products(thirds(vectors), w_in_t)
    gain_w, const_w = vectors_w[0], vectors_w[1] + b_in

    hidden, gain_w, const_w, w_out_t, *upstream_blocks = tie(
        hidden, gain_w, const_w, w_out_t, *upstream_blocks
    )
    scaled = (
        jnp.concatenate(upstream_blocks, axis=1).astype(F32) * scale_t
    ).astype(BF16)
    back_hidden = lax.dot_general(
        scaled, w_out_t, (((1,), (1,)), ((), ())), preferred_element_type=F32
    )
    back_pre = (back_hidden * act_slope).astype(BF16)
    back_wide = back_pre.astype(F32)
    cross = jnp.stack(
        [
            jnp.sum(back_wide * gain_w, axis=1),
            jnp.sum(back_wide * (preact - const_w), axis=1),
        ]
    )
    crosses = [cross] + [chan_shift(cross, k) for k in range(1, NCHAN)]

    def share(k, values):
        block = (NCHAN - k) % NCHAN
        weights = w_in_t[block * chan_dev : (block + 1) * chan_dev]
        return lax.dot_general(
            values, weights, (((1,), (1,)), ((), ())), preferred_element_type=F32
        )

    in_ours, in_theirs = weight_grad(ln_out, back_pre, factor)
    hidden, in_theirs, *crosses = tie(hidden, in_theirs, *crosses)
    in_arrived = core_swap(in_theirs)
    out_ours, out_theirs = weight_grad(scaled, hidden, factor)
    back_pre, out_theirs = tie(back_pre, out_theirs)
    out_arrived = core_swap(out_theirs)

    shares = [share(k, back_pre).astype(BF16) for k in (2, 1, 3)]
    back_pre, *shares = tie(back_pre, *shares)
    back_parts = [chan_shift(s, k) for s, k in zip(shares, (2, 1, 3))]
    back_own = share(0, back_pre)

    in_arrived, out_arrived, back_own = tie(in_arrived, out_arrived, back_own)

    def grouped(ours, theirs):
        kept = (ours.astype(F32) + theirs.astype(F32)).astype(BF16)
        return kept.reshape(NZ, NY, -1, kept.shape[1])

    kept = [grouped(in_ours, in_arrived), grouped(out_ours, out_arrived)]

    def get(k):
        at = (z + k) & (NZ - 1)
        place = ((chan - (at >> 1)) & (NCHAN - 1)) * 2 + (at & 1)
        return jnp.stack([pick(part, place, 0) for part in kept])

    def ring_step(distance, up, down):
        above = get(distance).astype(F32)
        below = get(-distance).astype(F32)
        if distance == far - 1:
            above = jnp.concatenate([above[:1] + up.astype(F32), above[1:]], axis=0)
            below = jnp.concatenate([below[:1], below[1:] + down.astype(F32)], axis=0)
        else:
            above = above + up.astype(F32)
            below = below + down.astype(F32)
        return above.astype(BF16), below.astype(BF16)

    far = NZ // 2
    chunk = get(far)
    up, down, back_own, *kept = tie(chunk[:1], chunk[1:], back_own, *kept)
    up, down = z_shift(up, 1), z_shift(down, -1)
    above, below = ring_step(3, up, down)
    above, below, back_own = tie(above, below, back_own)
    up, down = z_shift(above, 1), z_shift(below, -1)

    back_norm = back_own
    for part in back_parts:
        back_norm = back_norm + part.astype(F32)
    grad_normed = back_norm * ln_gain
    cross_sum = sum(crosses)
    sum_grad, sum_cross = cross_sum[0], cross_sum[1]
    grad_mixed = inv_std * (
        grad_normed - (sum_grad / C)[:, None] - normed * (sum_cross / C)[:, None]
    )
    grad_grid = grad_mixed.reshape(rows, PAGE_SIDE, chan_dev)
    taps = banded(
        functools.partial(taps_kernel, factor=factor),
        flags,
        band,
        (grad_grid,),
        jax.ShapeDtypeStruct((KSIZE * KSIZE, chan_dev), F32),
        (pltpu.VMEM((KSIZE * KSIZE, 8, LANES), F32),),
    )
    up, down, taps, grad_grid = tie(up, down, taps, grad_grid)
    above, below = ring_step(2, up, down)
    above, below, taps, grad_grid = tie(above, below, taps, grad_grid)
    up, down = z_shift(above, 1), z_shift(below, -1)

    def flip(axis, mask):
        pairs = []
        for zz in range(NZ):
            for yy in range(NY):
                for cc in range(NCORE):
                    mate = {
                        "z": (zz ^ mask, yy, cc), "y": (zz, yy ^ mask, cc), "c": (zz, yy, cc ^ mask)
                    }[axis]
                    pairs.append(
                        ((zz * NY + yy) * NCORE + cc, (mate[0] * NY + mate[1]) * NCORE + mate[2])
                    )
        return pairs

    def both(value, axis, mask):
        rounded = lax.reduce_precision(value, 8, 7)
        return rounded + lax.ppermute(rounded.astype(BF16), "tile", flip(axis, mask)).astype(F32)

    before, _, behind = edges(grad_grid.astype(BF16), reach)
    taps = taps + core_swap(taps)
    taps = both(taps, "y", 1)
    up, down, taps, before, behind = tie(up, down, taps, before, behind)
    above, below = ring_step(1, up, down)
    above, below, taps, before, behind = tie(above, below, taps, before, behind)
    up, down = z_shift(above, 1), z_shift(below, -1)
    grad_input = banded(
        functools.partial(conv_kernel, flipped=True),
        flags,
        (before, grad_grid, behind),
        (dw_kernel, upstream.reshape(rows, PAGE_SIDE, chan_dev)),
        jax.ShapeDtypeStruct((rows, PAGE_SIDE, chan_dev), BF16),
    ).reshape(tok_dev, chan_dev)
    taps = both(taps, "y", 2)
    taps = both(taps, "z", 1)
    up, down, taps, grad_input = tie(up, down, taps, grad_input)
    summed = get(0).astype(F32) + up.astype(F32) + down.astype(F32)
    y_parts = [y_shift(pick(summed, (y + k) & (NY - 1), 1).astype(BF16), k) for k in (1, 2, 3)]
    taps = both(taps, "z", 2)
    taps, *y_parts = tie(taps, *y_parts)
    grads = pick(summed, y, 1)
    for part in y_parts:
        grads = grads + part.astype(F32)
    grad_w_in, grad_w_out = grads[0], grads[1].T
    grad_kernel = both(taps, "z", 4)
    return (grad_input, grad_w_in, grad_w_out, grad_kernel)


def solution(mesh):
    placed = (
        P("tile", "chan"),
        P("tile"),
        P("tile", "chan"),
        P(None, "chan"),
        P("chan"),
        P("chan"),
        P(None, "chan"),
        P("chan"),
        P("chan", None),
        P(),
    )
    return jax.shard_map(
        shards,
        mesh=mesh,
        in_specs=placed,
        out_specs=(P("tile", "chan"), P("tile", "chan"), P("chan", "tile"), P(None, "chan")),
        check_vma=False,
    )
```

```python
import functools
import math

import jax
import jax.numpy as jnp
from jax import lax
from jax.experimental import pallas as pl
from jax.experimental.pallas import tpu as pltpu
from jax.sharding import PartitionSpec as P

C = 1536
KSIZE = 7
PAGE_SIDE = 48
EPS = 1e-06
NZ, NY, NCORE, NCHAN = 8, 4, 2, 4
BF16 = jnp.bfloat16
F32 = jnp.float32


def tile_shift(value, dz, dy, dc):
    pairs = []
    for z in range(NZ):
        for y in range(NY):
            for c in range(NCORE):
                source = (z * NY + y) * NCORE + c
                target = ((z + dz) % NZ * NY + (y + dy) % NY) * NCORE + (c + dc) % NCORE
                pairs.append((source, target))
    return lax.ppermute(value, "tile", pairs)


def chan_shift(value, step):
    return lax.ppermute(value, "chan", [(i, (i + step) % NCHAN) for i in range(NCHAN)])


def z_shift(value, step):
    return tile_shift(value, step, 0, 0)


def y_shift(value, step):
    return tile_shift(value, 0, step, 0)


def core_swap(value):
    return tile_shift(value, 0, 0, 1)


def edges(value, width):
    peers = NZ * NY * NCORE
    up = [(i, (i + 1) % peers) for i in range(peers)]
    down = [(j, i) for i, j in up]
    before = lax.ppermute(value[-width:], "tile", up)
    after = lax.ppermute(value[:width], "tile", down)
    return before, value, after


def gelu_parts(preact):
    normal_cdf = 0.5 * (1.0 + jax.scipy.special.erf(preact * 0.7071067811865476))
    density = jnp.exp(-0.5 * preact * preact) * 0.3989422804014327
    return (preact * normal_cdf, normal_cdf + preact * density)


LANES = 128
MARGIN = 8


def stage_windows(flags_ref, before_ref, own_ref, after_ref, pad, shifted):
    rows, cols, reach = own_ref.shape[0], own_ref.shape[1], KSIZE // 2
    pad[:, :MARGIN] = jnp.zeros((pad.shape[0], MARGIN, LANES), F32)
    pad[:, MARGIN + cols :] = jnp.zeros((pad.shape[0], MARGIN, LANES), F32)
    inside = slice(MARGIN, MARGIN + cols)
    pad[:reach, inside] = jnp.where(flags_ref[0] == 1, 0.0, before_ref[...].astype(F32))
    pad[reach : reach + rows, inside] = own_ref[...].astype(F32)
    pad[reach + rows :, inside] = jnp.where(flags_ref[1] == 1, 0.0, after_ref[...].astype(F32))
    for col_off in range(KSIZE):
        start = MARGIN - reach + col_off
        shifted[col_off] = pad[:, start : start + cols]


def conv_kernel(flags_ref, before_ref, own_ref, after_ref, taps_ref, *rest, flipped):
    *extra, out_ref, pad, shifted = rest
    stage_windows(flags_ref, before_ref, own_ref, after_ref, pad, shifted)
    rows, cols = own_ref.shape[0], own_ref.shape[1]
    group = 4

    def body(index, carry):
        first = index * group
        sums = [jnp.zeros((cols, LANES), F32)] * group
        for col_off in range(KSIZE):
            for line in range(group + KSIZE - 1):
                window = shifted[col_off, first + line]
                for row in range(group):
                    row_off = line - row
                    if 0 <= row_off < KSIZE:
                        tap = row_off * KSIZE + col_off
                        tap = KSIZE * KSIZE - 1 - tap if flipped else tap
                        sums[row] = sums[row] + taps_ref[tap : tap + 1, :] * window
        for row in range(group):
            value = sums[row]
            for ref in extra:
                value = value + ref[first + row].astype(F32)
            out_ref[first + row] = value.astype(out_ref.dtype)
        return carry

    lax.fori_loop(0, rows // group, body, 0)


def taps_kernel(flags_ref, before_ref, own_ref, after_ref, grad_ref, out_ref, pad, shifted, held, *, factor):
    stage_windows(flags_ref, before_ref, own_ref, after_ref, pad, shifted)
    rows, cols = own_ref.shape[0], own_ref.shape[1]
    group = 2
    held[...] = jnp.zeros(held.shape, F32)

    def body(index, carry):
        first = index * group
        grads = [grad_ref[first + row] for row in range(group)]
        for row_off in range(KSIZE):
            for col_off in range(KSIZE):
                value = shifted[col_off, first + row_off] * grads[0]
                for row in range(1, group):
                    value = value + shifted[col_off, first + row + row_off] * grads[row]
                tap = row_off * KSIZE + col_off
                held[tap] = held[tap] + jnp.sum(value.reshape(cols // 8, 8, LANES), axis=0)
        return carry

    lax.fori_loop(0, rows // group, body, 0)
    out_ref[...] = jnp.sum(held[...], axis=1) * factor


def banded(kernel, flags, band, others, out_shape, scratch=()):
    before, own, after_rows = band

    def spec(shape):
        index = (0,) * (len(shape) - 1)
        return pl.BlockSpec(shape[:-1] + (LANES,), lambda i: index + (i,))

    rows, cols, width = own.shape
    height = rows + 2 * (KSIZE // 2)
    return pl.pallas_call(
        kernel,
        out_shape=out_shape,
        grid=(width // LANES,),
        in_specs=[pl.BlockSpec(memory_space=pltpu.SMEM)]
        + [spec(v.shape) for v in (before, own, after_rows, *others)],
        out_specs=spec(out_shape.shape),
        scratch_shapes=[
            pltpu.VMEM((height, cols + 2 * MARGIN, LANES), F32),
            pltpu.VMEM((KSIZE, height, cols, LANES), F32),
            *scratch,
        ],
        compiler_params=pltpu.CompilerParams(vmem_limit_bytes=32 * 1024 * 1024),
        cost_estimate=pl.CostEstimate(flops=1000, bytes_accessed=1000, transcendentals=0),
    )(flags, before, own, after_rows, *others)


def tie(*values):
    return lax.optimization_barrier(values)


def thirds(value):
    high = lax.reduce_precision(value, 8, 7)
    middle = lax.reduce_precision(value - high, 8, 7)
    low = value - high - middle
    return jnp.concatenate([high, middle, low], axis=0).astype(BF16)


def joined(parts):
    rows = parts.shape[0] // 3
    high, middle, low = (parts[i * rows : (i + 1) * rows].astype(F32) for i in range(3))
    return high + (middle + low)


def joined_products(parts, weights):
    return joined(jnp.dot(parts, weights, preferred_element_type=F32))


def pick(value, index, axis):
    return lax.dynamic_index_in_dim(
        value, index, axis, keepdims=False, allow_negative_indices=False
    )


def grads_kernel(left_ref, right_ref, ours_ref, theirs_ref, *, factor, rows):
    core = lax.axis_index("tile") & (NCORE - 1)
    grad = factor * lax.dot_general(
        left_ref[...], right_ref[...], (((0,), (0,)), ((), ())), preferred_element_type=F32
    )
    grad = grad.reshape(-1, NCORE, rows, grad.shape[1])
    first, second = grad[:, 0].reshape(ours_ref.shape), grad[:, 1].reshape(ours_ref.shape)
    ours_ref[...] = jnp.where(core == 0, first, second).astype(BF16)
    theirs_ref[...] = jnp.where(core == 0, second, first).astype(BF16)


def weight_grad(left, right, factor):
    tokens, width = left.shape
    block = width // NCHAN
    rows = width // (NZ * NY * NCORE)
    out = jax.ShapeDtypeStruct((width // NCORE, width), BF16)
    half = pl.BlockSpec((block // NCORE, width), lambda i: (i, 0))
    return pl.pallas_call(
        functools.partial(grads_kernel, factor=factor, rows=rows),
        out_shape=(out, out),
        grid=(NCHAN,),
        in_specs=[
            pl.BlockSpec((tokens, block), lambda i: (0, i)),
            pl.BlockSpec((tokens, width), lambda i: (0, 0)),
        ],
        out_specs=(half, half),
        compiler_params=pltpu.CompilerParams(vmem_limit_bytes=32 * 1024 * 1024),
        cost_estimate=pl.CostEstimate(flops=1000, bytes_accessed=1000, transcendentals=0),
    )(left, right)


def shards(
    seq_grad, token_slot, pixels, dw_kernel, ln_gain, ln_bias, w_in, b_in, w_out, layer_scale
):
    tiles = NZ * NY * NCORE
    position = lax.axis_index("tile")
    chan = lax.axis_index("chan")
    z, y = position >> 3, (position >> 1) & (NY - 1)
    band_index = (position + 1) & (tiles - 1)
    slots = seq_grad.shape[0]
    capacity = slots // tiles
    tok_dev, chan_dev = pixels.shape
    reach = KSIZE // 2
    rows = tok_dev // PAGE_SIDE
    page_part = band_index & (PAGE_SIDE // rows - 1)
    flags = jnp.stack([page_part == 0, page_part == PAGE_SIDE // rows - 1]).astype(jnp.int32)
    factor = 1.0 / math.sqrt(tok_dev * tiles)

    band = edges(pixels.reshape(rows, PAGE_SIDE, chan_dev), reach)
    source = token_slot // slots
    local_slot = token_slot - source * slots
    ids = jnp.arange(tok_dev, dtype=jnp.int32)
    same = (source[:, None] == source[None, :]) & (ids[:, None] < ids[None, :])
    seat = source * capacity + jnp.sum(same.astype(jnp.int32), axis=0)
    seats = jnp.arange(slots, dtype=jnp.int32)
    request = jnp.sum(
        jnp.where(seat[:, None] == seats[None, :], local_slot[:, None] + 1, 0), axis=0
    )
    asked = lax.all_to_all(
        (request - 1).reshape(tiles, capacity), "tile", split_axis=0, concat_axis=0, tiled=True
    ).reshape(slots)
    found = jnp.dot(
        (asked[:, None] == seats[None, :]).astype(BF16), seq_grad, preferred_element_type=F32
    ).astype(BF16)
    found, *band = tie(found, *band)
    arrived = lax.all_to_all(
        found.reshape(tiles, capacity * 3, chan_dev // 3),
        "tile",
        split_axis=0,
        concat_axis=0,
        tiled=True,
    ).reshape(slots, chan_dev)

    mixed = banded(
        functools.partial(conv_kernel, flipped=False),
        flags,
        band,
        (dw_kernel,),
        jax.ShapeDtypeStruct((rows, PAGE_SIDE, chan_dev), F32),
    ).reshape(tok_dev, chan_dev)
    own_sum = jnp.sum(mixed, axis=1)
    local = mixed - (own_sum / chan_dev)[:, None]
    own_spread = jnp.sum(local * local, axis=1)
    extra = tok_dev - chan_dev
    message = jnp.stack(
        [own_sum, own_spread, jnp.pad(ln_gain, (0, extra)), jnp.pad(ln_bias, (0, extra))]
    )
    packed = thirds(message).reshape(-1, chan_dev)
    sent = jnp.concatenate([local.astype(BF16), packed], axis=0)
    received = [chan_shift(sent, k) for k in range(1, NCHAN)]

    upstream = jnp.dot(
        (seat[:, None] == seats[None, :]).astype(BF16), arrived, preferred_element_type=F32
    ).astype(BF16)
    upstream, w_in, w_out = tie(upstream, w_in, w_out)
    from_left, from_right = chan_shift(upstream, 1), chan_shift(upstream, -1)
    upstream, *received = tie(upstream, *received)
    w_out, from_left, from_right = tie(w_out, from_left, from_right)

    def turned(value, axis):
        return jnp.concatenate(
            [
                lax.dynamic_slice_in_dim(
                    value,
                    ((chan - k) & (NCHAN - 1)) * chan_dev,
                    chan_dev,
                    axis=axis,
                    allow_negative_indices=False,
                )
                for k in range(NCHAN)
            ],
            axis=axis,
        )

    w_in_t = turned(w_in, 0)
    scale_t = turned(layer_scale, 0)

    locals_ = [local] + [r[:tok_dev] for r in received]
    messages = [message] + [
        joined(r[tok_dev:].reshape(3 * message.shape[0], -1)) for r in received
    ]
    mean = sum(m[0] for m in messages) / C
    offsets = [m[0] / chan_dev - mean for m in messages]
    spread = sum(m[1] + chan_dev * (d * d) for m, d in zip(messages, offsets))
    inv_std = lax.rsqrt(spread / C + EPS)[:, None]
    gains = [m[2, :chan_dev] for m in messages]
    biases = [m[3, :chan_dev] for m in messages]
    normed = (local + offsets[0][:, None]) * inv_std
    ln_out = jnp.concatenate(
        [
            ((v.astype(F32) + d[:, None]) * inv_std * g + b).astype(BF16)
            for v, d, g, b in zip(locals_, offsets, gains, biases)
        ],
        axis=1,
    )
    ln_out, from_left, from_right = tie(ln_out, from_left, from_right)
    half_rows = tok_dev // 2
    across = jnp.concatenate(
        [chan_shift(from_left[:half_rows], 1), chan_shift(from_right[half_rows:], -1)], axis=0
    )
    upstream_blocks = [upstream, from_left, across, from_right]
    preact = jnp.dot(ln_out, w_in_t, preferred_element_type=F32) + b_in
    act_val, act_slope = gelu_parts(preact)
    hidden = act_val.astype(BF16)
    w_out_t = turned(w_out, 1)
    vectors = jnp.stack([jnp.concatenate(gains), jnp.concatenate(biases)])
    vectors_w = joined_products(thirds(vectors), w_in_t)
    gain_w, const_w = vectors_w[0], vectors_w[1] + b_in

    hidden, gain_w, const_w, w_out_t, *upstream_blocks = tie(
        hidden, gain_w, const_w, w_out_t, *upstream_blocks
    )
    scaled = (
        jnp.concatenate(upstream_blocks, axis=1).astype(F32) * scale_t
    ).astype(BF16)
    back_hidden = lax.dot_general(
        scaled, w_out_t, (((1,), (1,)), ((), ())), preferred_element_type=F32
    )
    back_pre = (back_hidden * act_slope).astype(BF16)
    back_wide = back_pre.astype(F32)
    cross = jnp.stack(
        [
            jnp.sum(back_wide * gain_w, axis=1),
            jnp.sum(back_wide * (preact - const_w), axis=1),
        ]
    )
    crosses = [cross] + [chan_shift(cross, k) for k in range(1, NCHAN)]

    def share(k, values):
        block = (NCHAN - k) % NCHAN
        weights = w_in_t[block * chan_dev : (block + 1) * chan_dev]
        return lax.dot_general(
            values, weights, (((1,), (1,)), ((), ())), preferred_element_type=F32
        )

    in_ours, in_theirs = weight_grad(ln_out, back_pre, factor)
    hidden, in_theirs, *crosses = tie(hidden, in_theirs, *crosses)
    in_arrived = core_swap(in_theirs)
    out_ours, out_theirs = weight_grad(scaled, hidden, factor)
    back_pre, out_theirs = tie(back_pre, out_theirs)
    out_arrived = core_swap(out_theirs)

    shares = [share(k, back_pre).astype(BF16) for k in (2, 1, 3)]
    back_pre, *shares = tie(back_pre, *shares)
    back_parts = [chan_shift(s, k) for s, k in zip(shares, (2, 1, 3))]
    back_own = share(0, back_pre)

    in_arrived, out_arrived, back_own = tie(in_arrived, out_arrived, back_own)

    def grouped(ours, theirs):
        kept = (ours.astype(F32) + theirs.astype(F32)).astype(BF16)
        return kept.reshape(NZ, NY, -1, kept.shape[1])

    kept = [grouped(in_ours, in_arrived), grouped(out_ours, out_arrived)]

    def get(k):
        at = (z + k) & (NZ - 1)
        place = ((chan - (at >> 1)) & (NCHAN - 1)) * 2 + (at & 1)
        return jnp.stack([pick(part, place, 0) for part in kept])

    def ring_step(distance, up, down):
        above = get(distance).astype(F32)
        below = get(-distance).astype(F32)
        if distance == far - 1:
            above = jnp.concatenate([above[:1] + up.astype(F32), above[1:]], axis=0)
            below = jnp.concatenate([below[:1], below[1:] + down.astype(F32)], axis=0)
        else:
            above = above + up.astype(F32)
            below = below + down.astype(F32)
        return above.astype(BF16), below.astype(BF16)

    far = NZ // 2
    chunk = get(far)
    up, down, back_own, *kept = tie(chunk[:1], chunk[1:], back_own, *kept)
    up, down = z_shift(up, 1), z_shift(down, -1)
    above, below = ring_step(3, up, down)
    above, below, back_own = tie(above, below, back_own)
    up, down = z_shift(above, 1), z_shift(below, -1)

    back_norm = back_own
    for part in back_parts:
        back_norm = back_norm + part.astype(F32)
    grad_normed = back_norm * ln_gain
    cross_sum = sum(crosses)
    sum_grad, sum_cross = cross_sum[0], cross_sum[1]
    grad_mixed = inv_std * (
        grad_normed - (sum_grad / C)[:, None] - normed * (sum_cross / C)[:, None]
    )
    grad_grid = grad_mixed.reshape(rows, PAGE_SIDE, chan_dev)
    taps = banded(
        functools.partial(taps_kernel, factor=factor),
        flags,
        band,
        (grad_grid,),
        jax.ShapeDtypeStruct((KSIZE * KSIZE, chan_dev), F32),
        (pltpu.VMEM((KSIZE * KSIZE, 8, LANES), F32),),
    )
    taps = taps + core_swap(taps)
    up, down, taps, grad_grid = tie(up, down, taps, grad_grid)
    above, below = ring_step(2, up, down)
    above, below, taps, grad_grid = tie(above, below, taps, grad_grid)
    up, down = z_shift(above, 1), z_shift(below, -1)

    def flip(axis, mask):
        pairs = []
        for zz in range(NZ):
            for yy in range(NY):
                for cc in range(NCORE):
                    mate = {
                        "z": (zz ^ mask, yy, cc), "y": (zz, yy ^ mask, cc), "c": (zz, yy, cc ^ mask)
                    }[axis]
                    pairs.append(
                        ((zz * NY + yy) * NCORE + cc, (mate[0] * NY + mate[1]) * NCORE + mate[2])
                    )
        return pairs

    def both(value, axis, mask):
        rounded = lax.reduce_precision(value, 8, 7)
        return rounded + lax.ppermute(rounded.astype(BF16), "tile", flip(axis, mask)).astype(F32)

    before, _, behind = edges(grad_grid.astype(BF16), reach)
    taps = both(taps, "y", 1)
    taps = both(taps, "y", 2)
    taps = both(taps, "z", 1)
    up, down, taps, before, behind = tie(up, down, taps, before, behind)
    above, below = ring_step(1, up, down)
    above, below, taps, before, behind = tie(above, below, taps, before, behind)
    up, down = z_shift(above, 1), z_shift(below, -1)
    grad_input = banded(
        functools.partial(conv_kernel, flipped=True),
        flags,
        (before, grad_grid, behind),
        (dw_kernel, upstream.reshape(rows, PAGE_SIDE, chan_dev)),
        jax.ShapeDtypeStruct((rows, PAGE_SIDE, chan_dev), BF16),
    ).reshape(tok_dev, chan_dev)
    taps = both(taps, "z", 2)
    up, down, taps, grad_input = tie(up, down, taps, grad_input)
    summed = get(0).astype(F32) + up.astype(F32) + down.astype(F32)
    summed, taps = tie(summed, taps)
    y_parts = [y_shift(pick(summed, (y + k) & (NY - 1), 1).astype(BF16), k) for k in (1, 2, 3)]
    grads = pick(summed, y, 1)
    for part in y_parts:
        grads = grads + part.astype(F32)
    grad_w_in, grad_w_out = grads[0], grads[1].T
    grad_kernel = both(taps, "z", 4)
    return (grad_input, grad_w_in, grad_w_out, grad_kernel)


def solution(mesh):
    placed = (
        P("tile", "chan"),
        P("tile"),
        P("tile", "chan"),
        P(None, "chan"),
        P("chan"),
        P("chan"),
        P(None, "chan"),
        P("chan"),
        P("chan", None),
        P(),
    )
    return jax.shard_map(
        shards,
        mesh=mesh,
        in_specs=placed,
        out_specs=(P("tile", "chan"), P("tile", "chan"), P("chan", "tile"), P(None, "chan")),
        check_vma=False,
    )
```

```python
import functools
import math

import jax
import jax.numpy as jnp
from jax import lax
from jax.experimental import pallas as pl
from jax.experimental.pallas import tpu as pltpu
from jax.sharding import PartitionSpec as P

C = 1536
KSIZE = 7
PAGE_SIDE = 48
EPS = 1e-06
NZ, NY, NCORE, NCHAN = 8, 4, 2, 4
BF16 = jnp.bfloat16
F32 = jnp.float32


def tile_shift(value, dz, dy, dc):
    pairs = []
    for z in range(NZ):
        for y in range(NY):
            for c in range(NCORE):
                source = (z * NY + y) * NCORE + c
                target = ((z + dz) % NZ * NY + (y + dy) % NY) * NCORE + (c + dc) % NCORE
                pairs.append((source, target))
    return lax.ppermute(value, "tile", pairs)


def chan_shift(value, step):
    return lax.ppermute(value, "chan", [(i, (i + step) % NCHAN) for i in range(NCHAN)])


def z_shift(value, step):
    return tile_shift(value, step, 0, 0)


def y_shift(value, step):
    return tile_shift(value, 0, step, 0)


def core_swap(value):
    return tile_shift(value, 0, 0, 1)


def edges(value, width):
    peers = NZ * NY * NCORE
    up = [(i, (i + 1) % peers) for i in range(peers)]
    down = [(j, i) for i, j in up]
    before = lax.ppermute(value[-width:], "tile", up)
    after = lax.ppermute(value[:width], "tile", down)
    return before, value, after


def gelu_parts(preact):
    normal_cdf = 0.5 * (1.0 + jax.scipy.special.erf(preact * 0.7071067811865476))
    density = jnp.exp(-0.5 * preact * preact) * 0.3989422804014327
    return (preact * normal_cdf, normal_cdf + preact * density)


LANES = 128
MARGIN = 8


def stage_windows(flags_ref, before_ref, own_ref, after_ref, pad, shifted):
    rows, cols, reach = own_ref.shape[0], own_ref.shape[1], KSIZE // 2
    pad[:, :MARGIN] = jnp.zeros((pad.shape[0], MARGIN, LANES), F32)
    pad[:, MARGIN + cols :] = jnp.zeros((pad.shape[0], MARGIN, LANES), F32)
    inside = slice(MARGIN, MARGIN + cols)
    pad[:reach, inside] = jnp.where(flags_ref[0] == 1, 0.0, before_ref[...].astype(F32))
    pad[reach : reach + rows, inside] = own_ref[...].astype(F32)
    pad[reach + rows :, inside] = jnp.where(flags_ref[1] == 1, 0.0, after_ref[...].astype(F32))
    for col_off in range(KSIZE):
        start = MARGIN - reach + col_off
        shifted[col_off] = pad[:, start : start + cols]


def conv_kernel(flags_ref, before_ref, own_ref, after_ref, taps_ref, *rest, flipped):
    *extra, out_ref, pad, shifted = rest
    stage_windows(flags_ref, before_ref, own_ref, after_ref, pad, shifted)
    rows, cols = own_ref.shape[0], own_ref.shape[1]
    group = 4

    def body(index, carry):
        first = index * group
        sums = [jnp.zeros((cols, LANES), F32)] * group
        for col_off in range(KSIZE):
            for line in range(group + KSIZE - 1):
                window = shifted[col_off, first + line]
                for row in range(group):
                    row_off = line - row
                    if 0 <= row_off < KSIZE:
                        tap = row_off * KSIZE + col_off
                        tap = KSIZE * KSIZE - 1 - tap if flipped else tap
                        sums[row] = sums[row] + taps_ref[tap : tap + 1, :] * window
        for row in range(group):
            value = sums[row]
            for ref in extra:
                value = value + ref[first + row].astype(F32)
            out_ref[first + row] = value.astype(out_ref.dtype)
        return carry

    lax.fori_loop(0, rows // group, body, 0)


def taps_kernel(flags_ref, before_ref, own_ref, after_ref, grad_ref, out_ref, pad, shifted, held, *, factor):
    stage_windows(flags_ref, before_ref, own_ref, after_ref, pad, shifted)
    rows, cols = own_ref.shape[0], own_ref.shape[1]
    group = 2
    held[...] = jnp.zeros(held.shape, F32)

    def body(index, carry):
        first = index * group
        grads = [grad_ref[first + row] for row in range(group)]
        for row_off in range(KSIZE):
            for col_off in range(KSIZE):
                value = shifted[col_off, first + row_off] * grads[0]
                for row in range(1, group):
                    value = value + shifted[col_off, first + row + row_off] * grads[row]
                tap = row_off * KSIZE + col_off
                held[tap] = held[tap] + jnp.sum(value.reshape(cols // 8, 8, LANES), axis=0)
        return carry

    lax.fori_loop(0, rows // group, body, 0)
    out_ref[...] = jnp.sum(held[...], axis=1) * factor


def banded(kernel, flags, band, others, out_shape, scratch=()):
    before, own, after_rows = band

    def spec(shape):
        index = (0,) * (len(shape) - 1)
        return pl.BlockSpec(shape[:-1] + (LANES,), lambda i: index + (i,))

    rows, cols, width = own.shape
    height = rows + 2 * (KSIZE // 2)
    return pl.pallas_call(
        kernel,
        out_shape=out_shape,
        grid=(width // LANES,),
        in_specs=[pl.BlockSpec(memory_space=pltpu.SMEM)]
        + [spec(v.shape) for v in (before, own, after_rows, *others)],
        out_specs=spec(out_shape.shape),
        scratch_shapes=[
            pltpu.VMEM((height, cols + 2 * MARGIN, LANES), F32),
            pltpu.VMEM((KSIZE, height, cols, LANES), F32),
            *scratch,
        ],
        compiler_params=pltpu.CompilerParams(vmem_limit_bytes=32 * 1024 * 1024),
        cost_estimate=pl.CostEstimate(flops=1000, bytes_accessed=1000, transcendentals=0),
    )(flags, before, own, after_rows, *others)


def tie(*values):
    return lax.optimization_barrier(values)


def thirds(value):
    high = lax.reduce_precision(value, 8, 7)
    middle = lax.reduce_precision(value - high, 8, 7)
    low = value - high - middle
    return jnp.concatenate([high, middle, low], axis=0).astype(BF16)


def joined(parts):
    rows = parts.shape[0] // 3
    high, middle, low = (parts[i * rows : (i + 1) * rows].astype(F32) for i in range(3))
    return high + (middle + low)


def joined_products(parts, weights):
    return joined(jnp.dot(parts, weights, preferred_element_type=F32))


def pick(value, index, axis):
    return lax.dynamic_index_in_dim(
        value, index, axis, keepdims=False, allow_negative_indices=False
    )


def grads_kernel(left_ref, right_ref, ours_ref, theirs_ref, *, rows):
    core = lax.axis_index("tile") & (NCORE - 1)
    grad = lax.dot_general(
        left_ref[...], right_ref[...], (((0,), (0,)), ((), ())), preferred_element_type=F32
    )
    grad = grad.reshape(-1, NCORE, rows, grad.shape[1])
    first, second = grad[:, 0].reshape(ours_ref.shape), grad[:, 1].reshape(ours_ref.shape)
    ours_ref[...] = jnp.where(core == 0, first, second).astype(BF16)
    theirs_ref[...] = jnp.where(core == 0, second, first).astype(BF16)


def weight_grad(left, right):
    tokens, width = left.shape
    block = width // NCHAN
    rows = width // (NZ * NY * NCORE)
    out = jax.ShapeDtypeStruct((width // NCORE, width), BF16)
    half = pl.BlockSpec((block // NCORE, width), lambda i: (i, 0))
    return pl.pallas_call(
        functools.partial(grads_kernel, rows=rows),
        out_shape=(out, out),
        grid=(NCHAN,),
        in_specs=[
            pl.BlockSpec((tokens, block), lambda i: (0, i)),
            pl.BlockSpec((tokens, width), lambda i: (0, 0)),
        ],
        out_specs=(half, half),
        compiler_params=pltpu.CompilerParams(vmem_limit_bytes=32 * 1024 * 1024),
        cost_estimate=pl.CostEstimate(flops=1000, bytes_accessed=1000, transcendentals=0),
    )(left, right)


def shards(
    seq_grad, token_slot, pixels, dw_kernel, ln_gain, ln_bias, w_in, b_in, w_out, layer_scale
):
    tiles = NZ * NY * NCORE
    position = lax.axis_index("tile")
    chan = lax.axis_index("chan")
    z, y = position >> 3, (position >> 1) & (NY - 1)
    band_index = (position + 1) & (tiles - 1)
    slots = seq_grad.shape[0]
    capacity = slots // tiles
    tok_dev, chan_dev = pixels.shape
    reach = KSIZE // 2
    rows = tok_dev // PAGE_SIDE
    page_part = band_index & (PAGE_SIDE // rows - 1)
    flags = jnp.stack([page_part == 0, page_part == PAGE_SIDE // rows - 1]).astype(jnp.int32)
    factor = 1.0 / math.sqrt(tok_dev * tiles)

    band = edges(pixels.reshape(rows, PAGE_SIDE, chan_dev), reach)
    source = token_slot // slots
    local_slot = token_slot - source * slots
    ids = jnp.arange(tok_dev, dtype=jnp.int32)
    same = (source[:, None] == source[None, :]) & (ids[:, None] < ids[None, :])
    seat = source * capacity + jnp.sum(same.astype(jnp.int32), axis=0)
    seats = jnp.arange(slots, dtype=jnp.int32)
    request = jnp.sum(
        jnp.where(seat[:, None] == seats[None, :], local_slot[:, None] + 1, 0), axis=0
    )
    asked = lax.all_to_all(
        (request - 1).reshape(tiles, capacity), "tile", split_axis=0, concat_axis=0, tiled=True
    ).reshape(slots)
    found = jnp.dot(
        (asked[:, None] == seats[None, :]).astype(BF16), seq_grad, preferred_element_type=F32
    ).astype(BF16)
    found, *band = tie(found, *band)
    arrived = lax.all_to_all(
        found.reshape(tiles, capacity * 3, chan_dev // 3),
        "tile",
        split_axis=0,
        concat_axis=0,
        tiled=True,
    ).reshape(slots, chan_dev)

    mixed = banded(
        functools.partial(conv_kernel, flipped=False),
        flags,
        band,
        (dw_kernel,),
        jax.ShapeDtypeStruct((rows, PAGE_SIDE, chan_dev), F32),
    ).reshape(tok_dev, chan_dev)
    own_sum = jnp.sum(mixed, axis=1)
    local = mixed - (own_sum / chan_dev)[:, None]
    own_spread = jnp.sum(local * local, axis=1)
    extra = tok_dev - chan_dev
    message = jnp.stack(
        [own_sum, own_spread, jnp.pad(ln_gain, (0, extra)), jnp.pad(ln_bias, (0, extra))]
    )
    packed = thirds(message).reshape(-1, chan_dev)
    sent = jnp.concatenate([local.astype(BF16), packed], axis=0)
    received = [chan_shift(sent, k) for k in range(1, NCHAN)]

    upstream = jnp.dot(
        (seat[:, None] == seats[None, :]).astype(BF16), arrived, preferred_element_type=F32
    ).astype(BF16)
    upstream, w_in, w_out = tie(upstream, w_in, w_out)
    from_left, from_right = chan_shift(upstream, 1), chan_shift(upstream, -1)
    upstream, *received = tie(upstream, *received)
    w_out, from_left, from_right = tie(w_out, from_left, from_right)

    def turned(value, axis):
        return jnp.concatenate(
            [
                lax.dynamic_slice_in_dim(
                    value,
                    ((chan - k) & (NCHAN - 1)) * chan_dev,
                    chan_dev,
                    axis=axis,
                    allow_negative_indices=False,
                )
                for k in range(NCHAN)
            ],
            axis=axis,
        )

    w_in_t = turned(w_in, 0)
    scale_t = turned(layer_scale, 0)

    locals_ = [local] + [r[:tok_dev] for r in received]
    messages = [message] + [
        joined(r[tok_dev:].reshape(3 * message.shape[0], -1)) for r in received
    ]
    mean = sum(m[0] for m in messages) / C
    offsets = [m[0] / chan_dev - mean for m in messages]
    spread = sum(m[1] + chan_dev * (d * d) for m, d in zip(messages, offsets))
    inv_std = lax.rsqrt(spread / C + EPS)[:, None]
    gains = [m[2, :chan_dev] for m in messages]
    biases = [m[3, :chan_dev] for m in messages]
    normed = (local + offsets[0][:, None]) * inv_std
    ln_out = jnp.concatenate(
        [
            ((v.astype(F32) + d[:, None]) * inv_std * g + b).astype(BF16)
            for v, d, g, b in zip(locals_, offsets, gains, biases)
        ],
        axis=1,
    )
    ln_out, from_left, from_right = tie(ln_out, from_left, from_right)
    half_rows = tok_dev // 2
    across = jnp.concatenate(
        [chan_shift(from_left[:half_rows], 1), chan_shift(from_right[half_rows:], -1)], axis=0
    )
    upstream_blocks = [upstream, from_left, across, from_right]
    preact = jnp.dot(ln_out, w_in_t, preferred_element_type=F32) + b_in
    act_val, act_slope = gelu_parts(preact)
    hidden = act_val.astype(BF16)
    w_out_t = turned(w_out, 1)
    vectors = jnp.stack([jnp.concatenate(gains), jnp.concatenate(biases)])
    vectors_w = joined_products(thirds(vectors), w_in_t)
    gain_w, const_w = vectors_w[0], vectors_w[1] + b_in

    hidden, gain_w, const_w, w_out_t, *upstream_blocks = tie(
        hidden, gain_w, const_w, w_out_t, *upstream_blocks
    )
    scaled = (
        jnp.concatenate(upstream_blocks, axis=1).astype(F32) * scale_t
    ).astype(BF16)
    back_hidden = lax.dot_general(
        scaled, w_out_t, (((1,), (1,)), ((), ())), preferred_element_type=F32
    )
    back_pre = (back_hidden * act_slope).astype(BF16)
    back_wide = back_pre.astype(F32)
    cross = jnp.stack(
        [
            jnp.sum(back_wide * gain_w, axis=1),
            jnp.sum(back_wide * (preact - const_w), axis=1),
        ]
    )
    crosses = [cross] + [chan_shift(cross, k) for k in range(1, NCHAN)]

    def share(k, values):
        block = (NCHAN - k) % NCHAN
        weights = w_in_t[block * chan_dev : (block + 1) * chan_dev]
        return lax.dot_general(
            values, weights, (((1,), (1,)), ((), ())), preferred_element_type=F32
        )

    in_ours, in_theirs = weight_grad(ln_out, back_pre)
    hidden, in_theirs, *crosses = tie(hidden, in_theirs, *crosses)
    in_arrived = core_swap(in_theirs)
    out_ours, out_theirs = weight_grad(scaled, hidden)
    back_pre, out_theirs = tie(back_pre, out_theirs)
    out_arrived = core_swap(out_theirs)

    shares = [share(k, back_pre).astype(BF16) for k in (2, 1, 3)]
    back_pre, *shares = tie(back_pre, *shares)
    back_parts = [chan_shift(s, k) for s, k in zip(shares, (2, 1, 3))]
    in_arrived, out_arrived, back_pre = tie(in_arrived, out_arrived, back_pre)

    def grouped(ours, theirs):
        kept = (ours.astype(F32) + theirs.astype(F32)).astype(BF16)
        return kept.reshape(NZ, NY, -1, kept.shape[1])

    kept = [grouped(in_ours, in_arrived), grouped(out_ours, out_arrived)]

    def get(k):
        at = (z + k) & (NZ - 1)
        place = ((chan - (at >> 1)) & (NCHAN - 1)) * 2 + (at & 1)
        return jnp.stack([pick(part, place, 0) for part in kept])

    def ring_step(distance, up, down):
        above = get(distance).astype(F32)
        below = get(-distance).astype(F32)
        if distance == far - 1:
            above = jnp.concatenate([above[:1] + up.astype(F32), above[1:]], axis=0)
            below = jnp.concatenate([below[:1], below[1:] + down.astype(F32)], axis=0)
        else:
            above = above + up.astype(F32)
            below = below + down.astype(F32)
        return above.astype(BF16), below.astype(BF16)

    far = NZ // 2
    chunk = get(far)
    up, down, back_pre, *kept = tie(chunk[:1], chunk[1:], back_pre, *kept)
    back_own = share(0, back_pre)
    up, down = z_shift(up, 1), z_shift(down, -1)
    above, below = ring_step(3, up, down)
    above, below, back_own = tie(above, below, back_own)
    up, down = z_shift(above, 1), z_shift(below, -1)

    back_norm = back_own
    for part in back_parts:
        back_norm = back_norm + part.astype(F32)
    grad_normed = back_norm * ln_gain
    cross_sum = sum(crosses)
    sum_grad, sum_cross = cross_sum[0], cross_sum[1]
    grad_mixed = inv_std * (
        grad_normed - (sum_grad / C)[:, None] - normed * (sum_cross / C)[:, None]
    )
    grad_grid = grad_mixed.reshape(rows, PAGE_SIDE, chan_dev)
    taps = banded(
        functools.partial(taps_kernel, factor=factor),
        flags,
        band,
        (grad_grid,),
        jax.ShapeDtypeStruct((KSIZE * KSIZE, chan_dev), F32),
        (pltpu.VMEM((KSIZE * KSIZE, 8, LANES), F32),),
    )
    taps = taps + core_swap(taps)
    up, down, taps, grad_grid = tie(up, down, taps, grad_grid)
    above, below = ring_step(2, up, down)
    above, below, taps, grad_grid = tie(above, below, taps, grad_grid)
    up, down = z_shift(above, 1), z_shift(below, -1)

    def flip(axis, mask):
        pairs = []
        for zz in range(NZ):
            for yy in range(NY):
                for cc in range(NCORE):
                    mate = {
                        "z": (zz ^ mask, yy, cc), "y": (zz, yy ^ mask, cc), "c": (zz, yy, cc ^ mask)
                    }[axis]
                    pairs.append(
                        ((zz * NY + yy) * NCORE + cc, (mate[0] * NY + mate[1]) * NCORE + mate[2])
                    )
        return pairs

    def both(value, axis, mask):
        rounded = lax.reduce_precision(value, 8, 7)
        return rounded + lax.ppermute(rounded.astype(BF16), "tile", flip(axis, mask)).astype(F32)

    before, _, behind = edges(grad_grid.astype(BF16), reach)
    taps = both(taps, "y", 1)
    taps = both(taps, "y", 2)
    up, down, taps, before, behind = tie(up, down, taps, before, behind)
    above, below = ring_step(1, up, down)
    above, below, taps, before, behind = tie(above, below, taps, before, behind)
    up, down = z_shift(above, 1), z_shift(below, -1)
    grad_input = banded(
        functools.partial(conv_kernel, flipped=True),
        flags,
        (before, grad_grid, behind),
        (dw_kernel, upstream.reshape(rows, PAGE_SIDE, chan_dev)),
        jax.ShapeDtypeStruct((rows, PAGE_SIDE, chan_dev), BF16),
    ).reshape(tok_dev, chan_dev)
    taps, grad_input = tie(both(taps, "z", 1), grad_input)
    taps = both(taps, "z", 2)
    up, down, taps, grad_input = tie(up, down, taps, grad_input)
    summed = get(0).astype(F32) + up.astype(F32) + down.astype(F32)
    summed, taps = tie(summed, taps)
    y_parts = [y_shift(pick(summed, (y + k) & (NY - 1), 1).astype(BF16), k) for k in (1, 2, 3)]
    grads = pick(summed, y, 1)
    for part in y_parts:
        grads = grads + part.astype(F32)
    grads = grads * factor
    grad_w_in, grad_w_out = grads[0], grads[1].T
    grad_kernel = both(taps, "z", 4)
    return (grad_input, grad_w_in, grad_w_out, grad_kernel)


def solution(mesh):
    placed = (
        P("tile", "chan"),
        P("tile"),
        P("tile", "chan"),
        P(None, "chan"),
        P("chan"),
        P("chan"),
        P(None, "chan"),
        P("chan"),
        P("chan", None),
        P(),
    )
    return jax.shard_map(
        shards,
        mesh=mesh,
        in_specs=placed,
        out_specs=(P("tile", "chan"), P("tile", "chan"), P("chan", "tile"), P(None, "chan")),
        check_vma=False,
    )
```
